256 devices in a mesh: dp: 32 (over z_hi, y, core), own: 8 (over x, z_lo).
Axes of the slice: x: 4, y: 4, z: 8 (z_hi: 4, z_lo: 2; z = z_hi * 2 + z_lo), core: 2. Of those that a mesh axis runs over, the one named last changes fastest.
Arguments:
- activations: bfloat16 [16384, 4096], P('dp', 'own'), may hold values from -40 to 40
- out_grads: bfloat16 [16384, 16384], P('dp', 'own'), may hold values from -40 to 40
- moved_tiles: int32 [32, 8], P('dp', 'own'), may hold values 0 or 1
- stale_roots: bfloat16 [32, 2, 512, 4096], P('dp', None, None, 'own'), may hold values from -7 to 7
Outputs:
- update: bfloat16 [32, 512, 4096], P('dp', None, 'own')
- fresh_roots: bfloat16 [64, 2, 512, 4096], P('dp', None, None, 'own')
The draws below stay inside these ranges and needn't reach their ends.
All inputs are finite; a program needn't handle non-finite values. No bound on the sum of `moved_tiles` on one device may be relied on, other than what follows from the above.
Results may differ from the reference program's by a relative error of at most 0.025.
Values may be sent and summed in bfloat16 or wider, within the bound.
A program may use at most 128 MiB of HBM per device.

```python
import jax
import jax.numpy as jnp
from jax import lax

BS = 512
D = 4096
F_DEV = 2048
ITERS = 2
F = 16384
TOKENS = 16384
TILES = 32
N_DP = 32
N_OWN = 8


def ramped_values(key, rows, columns):
    key_scale, key_values = jax.random.split(key, 2)
    ramp_up = jnp.arange(columns, dtype=jnp.float32) / (columns - 1)
    spread = jax.random.uniform(key_scale, (columns,), jnp.float32)
    scales = 10.0 ** (0.5 * ramp_up + 0.5 * spread)
    values = jnp.clip(jax.random.normal(key_values, (rows, columns), jnp.float32), -4.0, 4.0)
    return values * scales


def draw_activations(key, part):
    key = jax.random.fold_in(key, 11)
    return ramped_values(key, TOKENS, D).astype(jnp.bfloat16)


def draw_out_grads(key, part):
    key = jax.random.fold_in(key, 12)
    return ramped_values(key, TOKENS, F).astype(jnp.bfloat16)


def draw_stale_roots(key, part):
    key = jax.random.fold_in(key, 13)
    key_noise, key_diagonal = jax.random.split(key, 2)
    tile_shape = (TILES, 2, N_OWN, BS, BS)
    noise_draw = jnp.clip(jax.random.normal(key_noise, tile_shape, jnp.float32), -4.0, 4.0)
    symmetric = (noise_draw + jnp.swapaxes(noise_draw, -1, -2)) * (0.35 / (2.0 * BS) ** 0.5)
    diagonal = 0.5 + jax.random.uniform(key_diagonal, (TILES, 2, N_OWN, BS), jnp.float32)
    blocks = symmetric + diagonal[..., None] * jnp.eye(BS, dtype=jnp.float32)
    return blocks.transpose(0, 1, 3, 2, 4).reshape(TILES, 2, BS, N_OWN * BS).astype(jnp.bfloat16)


def with_ends(drawn, key, smallest, top_value):
    extent = drawn.shape
    place = [jax.random.randint(jax.random.fold_in(key, axis), (), 0, extent[axis]) for axis in range(len(extent))]
    drawn = drawn.at[tuple(place)].set(smallest)
    longest = extent.index(max(extent))
    place[longest] = (place[longest] + 1) % extent[longest]
    return drawn.at[tuple(place)].set(top_value)


def setup_inputs(seed: int = 0) -> dict:
    splits = jax.random.split(jax.random.key(seed), 5)
    return {
        "activations": draw_activations(jax.random.fold_in(splits[4], 71), 0),
        "out_grads": draw_out_grads(jax.random.fold_in(splits[4], 71), 0),
        "moved_tiles": with_ends((jax.random.randint(splits[2], (TILES, N_OWN), 0, 2) < 1).astype(jnp.int32), jax.random.fold_in(splits[2], 1), 0, 1),
        "stale_roots": draw_stale_roots(jax.random.fold_in(splits[4], 71), 0),
    }


EPSILON = 1e-06
POWER = 4.0

def matmul_high(left_side, right_side):
    return jnp.matmul(left_side, right_side, precision=lax.Precision.HIGHEST)

def refresh_roots(grad_blocks):
    tile_size = grad_blocks.shape[-1]
    wide_blocks = grad_blocks.astype(jnp.float32)
    left_stat = jnp.einsum('kab,kcb->kac', wide_blocks, wide_blocks, precision=lax.Precision.HIGHEST)
    right_stat = jnp.einsum('kba,kbc->kac', wide_blocks, wide_blocks, precision=lax.Precision.HIGHEST)
    identity = jnp.eye(tile_size, dtype=jnp.float32)
    statistics = jnp.stack([left_stat, right_stat], axis=1) + EPSILON * identity
    frobenius = jnp.sqrt(lax.optimization_barrier(jnp.sum(statistics * statistics, axis=(2, 3), keepdims=True)))
    start_scale = (POWER + 1.0) / (2.0 * frobenius)
    matrix = start_scale * statistics
    inverse_root = jnp.zeros_like(matrix)
    for sweep in range(ITERS):
        factor = ((POWER + 1.0) * identity - matrix) / POWER
        if sweep == 0:
            inverse_root = start_scale ** (1.0 / POWER) * factor
        else:
            inverse_root = matmul_high(inverse_root, factor)
        if sweep + 1 < ITERS:
            squared = matmul_high(factor, factor)
            matrix = matmul_high(matmul_high(squared, squared), matrix)
    return inverse_root.astype(jnp.bfloat16)

def reference(activations, out_grads, moved_tiles, stale_roots):
    tok_dev = activations.shape[0] // N_DP
    row_blocks = D // BS
    col_blocks = F_DEV // BS
    tiles_dev = TILES // N_DP
    shard_inputs = activations.reshape(N_DP, tok_dev, D)
    shard_grads = out_grads.reshape(N_DP, tok_dev, F)

    def add_shard(running, shard_pair):
        partial_value = jnp.dot(shard_pair[0].T, shard_pair[1], preferred_element_type=jnp.float32) / TOKENS
        rounded = lax.optimization_barrier(partial_value.astype(jnp.bfloat16))
        return (running + rounded.astype(jnp.float32), None)
    grad_sum, _ = lax.scan(add_shard, jnp.zeros((D, F), jnp.float32), (shard_inputs, shard_grads))
    grad_tiles = grad_sum.astype(jnp.bfloat16)
    blocks = grad_tiles.reshape(row_blocks, BS, N_OWN, col_blocks, BS).transpose(0, 3, 2, 1, 4)
    blocks = blocks.reshape(TILES, N_OWN, BS, BS)
    stale_blocks = stale_roots.reshape(TILES, 2, BS, N_OWN, BS).transpose(0, 3, 1, 2, 4)
    left_stale = stale_blocks[:, :, 0].astype(jnp.float32)
    right_stale = stale_blocks[:, :, 1].astype(jnp.float32)
    left_applied = jnp.einsum('tjab,tjbc->tjac', left_stale, blocks.astype(jnp.float32), precision=lax.Precision.HIGHEST).astype(jnp.bfloat16)
    precond = jnp.einsum('tjab,tjbc->tjac', left_applied.astype(jnp.float32), right_stale, precision=lax.Precision.HIGHEST)
    norm_total = jnp.sum(precond * precond)
    entry_count = TILES * N_OWN * BS * BS
    update = (precond * lax.rsqrt(norm_total / entry_count + 1e-06)).astype(jnp.bfloat16)
    update = update.transpose(0, 2, 1, 3).reshape(TILES, BS, N_OWN * BS)
    new_roots = lax.map(refresh_roots, blocks)
    new_roots = new_roots.reshape(N_DP, tiles_dev, N_OWN, 2, BS, BS)
    move_flags = moved_tiles.astype(jnp.bfloat16).reshape(N_DP, tiles_dev, N_OWN, 1, 1, 1)
    kept_roots = new_roots * (jnp.ones_like(move_flags) - move_flags)
    moved_roots = jnp.roll(new_roots * move_flags, 1, axis=0)
    slot_roots = jnp.concatenate([kept_roots, moved_roots], axis=1)
    slot_roots = slot_roots.reshape(2 * TILES, N_OWN, 2, BS, BS).transpose(0, 2, 3, 1, 4)
    fresh_roots = slot_roots.reshape(2 * TILES, 2, BS, N_OWN * BS)
    return (update, fresh_roots)
```

```python
import functools

import jax
import jax.numpy as jnp
from jax import lax
from jax.experimental import pallas as pl
from jax.experimental.pallas import tpu as pltpu
from jax.sharding import PartitionSpec as P

N_DP = 32
N_OWN = 8
BS = 512
HALF = BS // 2
TOKENS = 16384
EPSILON = 1e-06
ENTRIES = N_DP * N_OWN * BS * BS

MESH = pl.DeviceIdType.MESH
F32 = jnp.float32
BF16 = jnp.bfloat16

X_ORDER = (0, 1, 3, 2)
Y_GROUPS = ((0, 1, 0, 512), (1, 1, 0, 512)) + tuple((2, 2, 128 * s, 128) for s in range(4))
Z_GROUPS = tuple((128 * s, 128) for s in range(4))

N_SEMS = 19 + 2 + 1 + len(Y_GROUPS) * 6 + len(Z_GROUPS) * 7 + 17


def dot(left, right, contract=(1, 0)):
    dims = (((contract[0],), (contract[1],)), ((), ()))
    return lax.dot_general(left, right, dims, preferred_element_type=F32)


def identity_rows(first_row, rows):
    row = lax.broadcasted_iota(jnp.int32, (rows, BS), 0) + first_row
    column = lax.broadcasted_iota(jnp.int32, (rows, BS), 1)
    return (row == column).astype(F32)


def kernel(
    act, grads, moved, stale,
    update, fresh,
    act_own, a_all, b_all, part,
    y_relay_lo, y_relay_hi, y_sum_lo, y_sum_hi, y_from_minus, y_from_plus,
    ysum,
    z_relay_lo, z_relay_hi, z_sum_lo, z_sum_hi, z_from_minus, z_from_plus,
    grad, grad_prev, flag, flag_prev, stale_v,
    left_applied, precond, stat, stat_b, mid_n, mid_e, mid_t, mid_tb,
    norm1, norm2, norm3,
    send_sems, recv_sems, local_sems,
):
    dp = lax.axis_index("dp")
    own = lax.axis_index("own")
    core = lax.rem(dp, 2)
    y = lax.rem(dp // 2, 4)
    z = dp // 8
    x = own // 2
    z_lo = lax.rem(own, 2)

    sibling = dp + 1 - 2 * core
    pair = own + 1 - 2 * z_lo
    x_plus, x_minus = lax.rem(own + 2, N_OWN), lax.rem(own + 6, N_OWN)

    def dp_y(by):
        return z * 8 + lax.rem(y + by, 4) * 2 + core

    def dp_low(by):
        return z * 8 + lax.rem(lax.rem(dp, 8) + by, 8)

    def dp_z(by):
        return lax.rem(dp + 8 * by, N_DP)

    def own_at(by):
        return lax.rem(own + by, N_OWN)

    sent = []
    counter = [0]

    def new_sem():
        counter[0] += 1
        return counter[0] - 1

    def send(n, src, dst, to_dp, to_own):
        copy = pltpu.make_async_remote_copy(
            src_ref=src, dst_ref=dst, send_sem=send_sems.at[n], recv_sem=recv_sems.at[n],
            device_id=(to_dp, to_own), device_id_type=MESH,
        )
        copy.start()
        sent.append(copy)

    def arrive(n, dst):
        pltpu.make_async_remote_copy(
            src_ref=dst, dst_ref=dst, send_sem=send_sems.at[n], recv_sem=recv_sems.at[n],
            device_id=(sibling, own), device_id_type=MESH,
        ).wait_recv()

    load_act = pltpu.make_async_copy(act, act_own, local_sems.at[0])
    load_act.start()
    load_b = []
    for ch in range(2):
        load = pltpu.make_async_copy(
            grads.at[:, pl.ds(pl.multiple_of((2 * ch + core) * BS, BS), BS)],
            b_all.at[ch, pl.ds(pl.multiple_of(core * BS, BS), BS), :],
            local_sems.at[1 + ch],
        )
        load.start()
        load_b.append(load)
    load_stale = pltpu.make_async_copy(stale, stale_v, local_sems.at[3])
    load_stale.start()

    cross = lax.rem(dp + 2 * core - 1 + N_DP, N_DP)
    barrier = pltpu.get_barrier_semaphore()
    partners = [(dp, own_at(i)) for i in range(1, 8)]
    partners += [(dp_low(i), own) for i in range(1, 8)]
    partners += [(dp_z(i), own) for i in range(1, 4)]
    partners += [(cross, own)]
    for partner in partners:
        pl.semaphore_signal(barrier, inc=1, device_id=partner, device_id_type=MESH)

    my_tokens = pl.ds(pl.multiple_of(core * BS, BS), BS)
    sib_tokens = pl.ds(pl.multiple_of((1 - core) * BS, BS), BS)
    load_act.wait()
    for i in range(4):
        a_all[own, i * 128:(i + 1) * 128, my_tokens] = act_own[:, i * 128:(i + 1) * 128].T
    flag[...] = jnp.full((8, 128), moved[0, 0].astype(F32))

    pl.semaphore_wait(barrier, len(partners))

    def block(r, tokens, half=None):
        if half is None:
            return a_all.at[r, :, tokens]
        return a_all.at[r, half * HALF:(half + 1) * HALF, tokens]

    n_flag = new_sem()
    n_b = [new_sem() for _ in range(2)]
    n_sib = {}

    def to_sibling(key, r, half=None):
        n_sib[key] = new_sem()
        send(n_sib[key], block(r, my_tokens, half), block(r, my_tokens, half), sibling, own)

    def from_sibling(key, r, half=None):
        arrive(n_sib[key], block(r, sib_tokens, half))

    n_pair = new_sem()
    send(n_pair, block(own, my_tokens), block(own, my_tokens), dp, pair)
    to_sibling("own", own)
    n_xp, n_xm = new_sem(), new_sem()
    send(n_xp, block(own, my_tokens), block(own, my_tokens), dp, x_plus)
    send(n_xm, block(own, my_tokens), block(own, my_tokens), dp, x_minus)
    for ch in range(2):
        send(
            n_b[ch],
            grads.at[:, pl.ds(pl.multiple_of((2 * ch + 1 - core) * BS, BS), BS)],
            b_all.at[ch, my_tokens, :],
            sibling, own,
        )
    next_dp = lax.rem(dp + 1, N_DP)
    send(n_flag, flag, flag_prev, next_dp, own)

    def products(r, slot):
        @pl.loop(0, 4)
        def _(i):
            ch = i // 2
            rows = pl.ds(pl.multiple_of(lax.rem(i, 2) * HALF, HALF), HALF)
            value = dot(a_all[r, rows, :], b_all[ch]) * (1.0 / TOKENS)
            target = lax.rem(lax.rem(r, 2) * 2 + ch - y + 4, 4)
            part[slot, target, rows, :] = value.astype(BF16)

    for load in load_b:
        load.wait()
    for ch in range(2):
        arrive(n_b[ch], b_all.at[ch, sib_tokens, :])
    from_sibling("own", own)
    products(own, 0)

    def tree_a(src, relay_lo, relay_hi, from_minus, from_plus, to_plus, to_minus, sems):
        send(sems[0], src(2, 0), relay_lo, *to_plus)
        send(sems[1], src(2, 1), relay_hi, *to_minus)
        send(sems[2], src(1, 1), from_minus(1), *to_plus)
        send(sems[3], src(3, 0), from_plus(0), *to_minus)

    def y_views(group):
        first, many, column, columns = Y_GROUPS[group]
        cols = slice(column, column + columns)
        slots = slice(first, first + many)

        def src(rho, half):
            return part.at[slots, rho, half * HALF:(half + 1) * HALF, cols]

        def half_of(ref):
            return lambda half: ref.at[slots, half * HALF:(half + 1) * HALF, cols]

        def piece(ref):
            return ref.at[slots, :, cols]

        return src, half_of, piece

    y_sems = [[new_sem() for _ in range(6)] for _ in Y_GROUPS]
    z_sems = [[new_sem() for _ in range(6)] for _ in Z_GROUPS]
    to_y = ((dp_y(1), own), (dp_y(3), own))
    to_z = ((dp_z(1), own), (dp_z(3), own))

    def y_a(group):
        src, half_of, piece = y_views(group)
        tree_a(src, piece(y_relay_lo), piece(y_relay_hi), half_of(y_from_minus),
               half_of(y_from_plus), *to_y, y_sems[group])

    def y_b(group):
        src, half_of, piece = y_views(group)
        sems = y_sems[group]
        arrive(sems[0], piece(y_relay_lo))
        piece(y_sum_lo)[...] = src(1, 0)[...] + piece(y_relay_lo)[...]
        send(sems[4], piece(y_sum_lo), half_of(y_from_minus)(0), *to_y[0])
        arrive(sems[1], piece(y_relay_hi))
        piece(y_sum_hi)[...] = src(3, 1)[...] + piece(y_relay_hi)[...]
        send(sems[5], piece(y_sum_hi), half_of(y_from_plus)(1), *to_y[1])

    def y_c(group):
        src, half_of, piece = y_views(group)
        sems = y_sems[group]
        arrive(sems[2], half_of(y_from_minus)(1))
        arrive(sems[3], half_of(y_from_plus)(0))
        arrive(sems[4], half_of(y_from_minus)(0))
        arrive(sems[5], half_of(y_from_plus)(1))
        first, many, column, columns = Y_GROUPS[group]
        cols = slice(column, column + columns)
        for slot in range(first, first + many):
            target = lax.rem(x + X_ORDER[slot] - z + 4, 4)
            total = part[slot, 0, :, cols].astype(F32) + y_from_minus[slot, :, cols].astype(F32)
            total = total + y_from_plus[slot, :, cols].astype(F32)
            ysum[target, :, cols] = total.astype(BF16)

    def z_views(group):
        column, columns = Z_GROUPS[group]
        cols = slice(column, column + columns)

        def src(rho, half):
            return ysum.at[rho, half * HALF:(half + 1) * HALF, cols]

        def half_of(ref):
            return lambda half: ref.at[half * HALF:(half + 1) * HALF, cols]

        def piece(ref):
            return ref.at[:, cols]

        return src, half_of, piece

    def z_a(group):
        src, half_of, piece = z_views(group)
        tree_a(src, piece(z_relay_lo), piece(z_relay_hi), half_of(z_from_minus),
               half_of(z_from_plus), *to_z, z_sems[group])

    def z_b(group):
        src, half_of, piece = z_views(group)
        sems = z_sems[group]
        arrive(sems[0], piece(z_relay_lo))
        piece(z_sum_lo)[...] = src(1, 0)[...] + piece(z_relay_lo)[...]
        send(sems[4], piece(z_sum_lo), half_of(z_from_minus)(0), *to_z[0])
        arrive(sems[1], piece(z_relay_hi))
        piece(z_sum_hi)[...] = src(3, 1)[...] + piece(z_relay_hi)[...]
        send(sems[5], piece(z_sum_hi), half_of(z_from_plus)(1), *to_z[1])

    grad_sems = [new_sem() for _ in Z_GROUPS]

    def z_c(group):
        src, half_of, piece = z_views(group)
        sems = z_sems[group]
        arrive(sems[2], half_of(z_from_minus)(1))
        arrive(sems[3], half_of(z_from_plus)(0))
        arrive(sems[4], half_of(z_from_minus)(0))
        arrive(sems[5], half_of(z_from_plus)(1))
        column, columns = Z_GROUPS[group]
        cols = slice(column, column + columns)
        total = ysum[0, :, cols].astype(F32) + z_from_minus[:, cols].astype(F32)
        total = total + z_from_plus[:, cols].astype(F32)
        grad[:, cols] = total.astype(BF16)
        send(grad_sems[group], grad.at[:, cols], grad_prev.at[:, cols], next_dp, own)

    arrive(n_pair, block(pair, my_tokens))
    to_sibling("pair", pair)
    n_xp2, n_xm2 = new_sem(), new_sem()
    send(n_xp2, block(pair, my_tokens), block(pair, my_tokens), dp, x_plus)
    send(n_xm2, block(pair, my_tokens), block(pair, my_tokens), dp, x_minus)
    from_sibling("pair", pair)
    products(pair, 0)
    y_a(0)

    pair_plus, pair_minus = lax.rem(pair + 2, N_OWN), lax.rem(pair + 6, N_OWN)
    far, pair_far = lax.rem(own + 4, N_OWN), lax.rem(pair + 4, N_OWN)
    arrive(n_xp, block(x_minus, my_tokens))
    to_sibling("minus", x_minus)
    n_far = {}
    n_far["own", 0] = new_sem()
    send(n_far["own", 0], block(x_minus, my_tokens, 0), block(x_minus, my_tokens, 0), dp, x_plus)
    arrive(n_xm, block(x_plus, my_tokens))
    to_sibling("plus", x_plus)
    n_far["own", 1] = new_sem()
    send(n_far["own", 1], block(x_plus, my_tokens, 1), block(x_plus, my_tokens, 1), dp, x_minus)
    from_sibling("plus", x_plus)
    products(x_plus, 1)
    from_sibling("minus", x_minus)
    products(x_minus, 2)
    y_b(0)

    arrive(n_xm2, block(pair_plus, my_tokens))
    to_sibling("pair_plus", pair_plus)
    n_far["pair", 1] = new_sem()
    send(n_far["pair", 1], block(pair_plus, my_tokens, 1), block(pair_plus, my_tokens, 1), dp, x_minus)
    arrive(n_xp2, block(pair_minus, my_tokens))
    to_sibling("pair_minus", pair_minus)
    n_far["pair", 0] = new_sem()
    send(n_far["pair", 0], block(pair_minus, my_tokens, 0), block(pair_minus, my_tokens, 0), dp, x_plus)
    from_sibling("pair_plus", pair_plus)
    products(pair_plus, 1)
    y_a(1)
    from_sibling("pair_minus", pair_minus)
    products(pair_minus, 2)
    y_c(0)

    for name, r in (("own", far), ("pair", pair_far)):
        for half in range(2):
            arrive(n_far[name, half], block(r, my_tokens, half))
            to_sibling(("far", name, half), r, half)
    y_b(1)
    for name, r in (("own", far), ("pair", pair_far)):
        for half in range(2):
            from_sibling(("far", name, half), r, half)
        products(r, 3)

    y_a(2)
    y_c(1)
    y_b(2)
    y_a(3)
    y_c(2)
    z_a(0)
    y_b(3)
    y_a(4)
    z_b(0)
    y_c(3)
    z_a(1)
    y_b(4)
    y_a(5)
    z_c(0)
    z_b(1)
    y_c(4)
    z_a(2)
    y_b(5)
    z_c(1)
    z_b(2)
    y_c(5)
    z_a(3)
    z_c(2)
    z_b(3)
    z_c(3)

    load_stale.wait()
    squares = jnp.zeros((1, 1), F32)
    for half in range(2):
        rows = slice(half * HALF, (half + 1) * HALF)
        left_applied[rows, :] = dot(stale_v[0, 0, rows, :], grad[...]).astype(BF16)
        value = dot(left_applied[rows, :], stale_v[0, 1])
        precond[rows, :] = value
        squares = squares + jnp.sum(value * value, keepdims=True)

    def spread(store, value, targets):
        store[0] = jnp.broadcast_to(value, (8, 128))
        sems = [new_sem() for _ in targets]
        for i, target in enumerate(targets):
            send(sems[i], store.at[0], store.at[i + 1], *target)
        return sems

    def collect(store, sems):
        for i, n in enumerate(sems):
            arrive(n, store.at[i + 1])
        return jnp.sum(store[...], axis=0)[0:1, 0:1]

    def root(tile, side, slot, keep):
        total = jnp.zeros((1, 1), F32)
        for half in range(2):
            rows = slice(half * HALF, (half + 1) * HALF)
            if side == 0:
                value = dot(tile[rows, :], tile[...], (1, 1))
            else:
                value = dot(tile[:, rows], tile[...], (0, 0))
            value = value + EPSILON * identity_rows(half * HALF, HALF)
            stat[rows, :] = value
            total = total + jnp.sum(value * value, keepdims=True)
        scale = 2.5 / jnp.sqrt(total)
        matrix = stat[...] * scale
        stat[...] = matrix
        stat_b[...] = matrix.astype(BF16)
        for half in range(2):
            rows = slice(half * HALF, (half + 1) * HALF)
            squared = dot(stat_b[rows, :], stat_b[...])
            matrix = stat[rows, :]
            mid_n[rows, :] = (5.0 * matrix - squared) * 0.25
            mid_e[rows, :] = ((squared - 10.0 * matrix) * 0.0625).astype(BF16)
        for half in range(2):
            rows = slice(half * HALF, (half + 1) * HALF)
            value = 1.5625 * mid_n[rows, :] + dot(mid_e[rows, :], mid_n[...].astype(BF16))
            mid_t[rows, :] = value
            mid_tb[rows, :] = value.astype(BF16)
        factor = jnp.sqrt(jnp.sqrt(scale)) * 0.25
        for half in range(2):
            rows = slice(half * HALF, (half + 1) * HALF)
            value = 1.5625 * mid_t[rows, :] + dot(mid_e[rows, :], mid_tb[...])
            first = (25.0 * identity_rows(half * HALF, HALF) - 5.0 * stat[rows, :]) * 0.25
            result = ((first - value) * factor).astype(BF16)
            fresh[slot, side, rows, :] = (result.astype(F32) * keep).astype(BF16)

    sems1 = spread(norm1, squares, [(dp, own_at(i)) for i in range(1, 8)])
    keep = 1.0 - flag[0:1, 0:1]
    root(grad, 0, 0, keep)
    sems2 = spread(norm2, collect(norm1, sems1), [(dp_low(i), own) for i in range(1, 8)])
    root(grad, 1, 0, keep)
    sems3 = spread(norm3, collect(norm2, sems2), [(dp_z(i), own) for i in range(1, 4)])
    arrive(n_flag, flag_prev)
    for group, (column, columns) in enumerate(Z_GROUPS):
        arrive(grad_sems[group], grad_prev.at[:, column:column + columns])
    keep = flag_prev[0:1, 0:1]
    root(grad_prev, 0, 1, keep)
    norm_total = collect(norm3, sems3)
    update[0] = (precond[...] * lax.rsqrt(norm_total / ENTRIES + 1e-06)).astype(BF16)
    root(grad_prev, 1, 1, keep)

    for copy in sent:
        copy.wait_send()
    assert counter[0] <= N_SEMS, counter[0]


def body(activations, out_grads, moved_tiles, stale_roots):
    tile = (BS, BS)
    half = (HALF, BS)
    scratch = [
        ((BS, BS), BF16),
        ((N_OWN, BS, 2 * BS), BF16),
        ((2, 2 * BS, BS), BF16),
        ((4, 4) + tile, BF16),
        ((4,) + half, BF16), ((4,) + half, BF16), ((4,) + half, BF16), ((4,) + half, BF16),
        ((4,) + tile, BF16), ((4,) + tile, BF16),
        ((4,) + tile, BF16),
        (half, BF16), (half, BF16), (half, BF16), (half, BF16), (tile, BF16), (tile, BF16),
        (tile, BF16), (tile, BF16), ((8, 128), F32), ((8, 128), F32), ((1, 2) + tile, BF16),
        (tile, BF16), (tile, F32), (tile, F32), (tile, BF16), (tile, F32), (tile, BF16),
        (tile, F32), (tile, BF16),
        ((8, 8, 128), F32), ((8, 8, 128), F32), ((4, 8, 128), F32),
    ]
    flops = 2 * 2 * 512 * 4096 * 2048
    return tuple(pl.pallas_call(
        kernel,
        out_shape=(
            jax.ShapeDtypeStruct((1, BS, BS), BF16),
            jax.ShapeDtypeStruct((2, 2, BS, BS), BF16),
        ),
        in_specs=[
            pl.BlockSpec(memory_space=pl.ANY),
            pl.BlockSpec(memory_space=pl.ANY),
            pl.BlockSpec(memory_space=pltpu.SMEM),
            pl.BlockSpec(memory_space=pl.ANY),
        ],
        out_specs=(pl.BlockSpec(memory_space=pltpu.VMEM), pl.BlockSpec(memory_space=pltpu.VMEM)),
        scratch_shapes=[pltpu.VMEM(shape, dtype) for shape, dtype in scratch] + [
            pltpu.SemaphoreType.DMA((N_SEMS,)),
            pltpu.SemaphoreType.DMA((N_SEMS,)),
            pltpu.SemaphoreType.DMA((4,)),
        ],
        compiler_params=pltpu.CompilerParams(
            collective_id=0, has_side_effects=True, vmem_limit_bytes=60 * 1024 * 1024
        ),
        cost_estimate=pl.CostEstimate(flops=flops, bytes_accessed=6 << 20, transcendentals=0),
    )(activations, out_grads, moved_tiles, stale_roots))


def solution(mesh):
    in_specs = (P("dp", "own"), P("dp", "own"), P("dp", "own"), P("dp", None, None, "own"))
    out_specs = (P("dp", None, "own"), P("dp", None, None, "own"))
    return jax.shard_map(body, mesh=mesh, in_specs=in_specs, out_specs=out_specs, check_vma=False)
```

```python
import functools

import jax
import jax.numpy as jnp
from jax import lax
from jax.experimental import pallas as pl
from jax.experimental.pallas import tpu as pltpu
from jax.sharding import PartitionSpec as P

N_DP = 32
N_OWN = 8
BS = 512
HALF = BS // 2
TOKENS = 16384
EPSILON = 1e-06
ENTRIES = N_DP * N_OWN * BS * BS

MESH = pl.DeviceIdType.MESH
F32 = jnp.float32
BF16 = jnp.bfloat16

X_ORDER = (0, 1, 3, 2)
SLICE = 128
SLICES = BS // SLICE
Y_PIECES = (
    (0, 1, 0, 128), (0, 1, 128, 128), (0, 1, 256, 128), (0, 1, 384, 128), (1, 3, 0, 128),
    (3, 4, 0, 128), (1, 4, 128, 64), (1, 4, 192, 64), (1, 4, 256, 64), (1, 4, 320, 64),
    (1, 4, 384, 64), (1, 4, 448, 64),
)
Z_PIECES = ((0, 64), (64, 64), (128, 64), (192, 64), (256, 64), (320, 64), (384, 64), (448, 64))

N_SEMS = 320


def dot(left, right, contract=(1, 0)):
    dims = (((contract[0],), (contract[1],)), ((), ()))
    return lax.dot_general(left, right, dims, preferred_element_type=F32)


def identity_rows(first_row, rows):
    row = lax.broadcasted_iota(jnp.int32, (rows, BS), 0) + first_row
    column = lax.broadcasted_iota(jnp.int32, (rows, BS), 1)
    return (row == column).astype(F32)


def kernel(
    act, grads, moved, stale,
    precond_out, fresh_out, norm_out,
    a_all, b_all, part,
    y_relay, y_sum, y_from_minus, y_from_plus,
    ysum,
    z_relay, z_sum, z_from_minus, z_from_plus,
    grad, grad_prev, flag, flag_prev, stale_v,
    left_applied, precond, stat, stat_b, mid_n, mid_e, mid_t, mid_tb,
    norm1, norm2, fresh,
    send_sems, recv_sems, local_sems,
):
    dp = lax.axis_index("dp")
    own = lax.axis_index("own")
    core = lax.rem(dp, 2)
    y = lax.rem(dp // 2, 4)
    z = dp // 8
    x = own // 2
    z_lo = lax.rem(own, 2)

    sibling = dp + 1 - 2 * core
    pair = own + 1 - 2 * z_lo
    x_plus, x_minus = lax.rem(own + 2, N_OWN), lax.rem(own + 6, N_OWN)

    def dp_y(by):
        return z * 8 + lax.rem(y + by, 4) * 2 + core

    def dp_at(by):
        return lax.rem(dp + by, N_DP)

    def dp_z(by):
        return dp_at(8 * by)

    def own_at(by):
        return lax.rem(own + by, N_OWN)

    sent = []
    counter = [0]
    my_tokens = pl.ds(pl.multiple_of(core * BS, BS), BS)
    sib_tokens = pl.ds(pl.multiple_of((1 - core) * BS, BS), BS)

    def new_sem():
        counter[0] += 1
        return counter[0] - 1

    def send(n, src, dst, to_dp, to_own, keep=True):
        copy = pltpu.make_async_remote_copy(
            src_ref=src, dst_ref=dst, send_sem=send_sems.at[n], recv_sem=recv_sems.at[n],
            device_id=(to_dp, to_own), device_id_type=MESH,
        )
        copy.start()
        if keep:
            sent.append((n, src.shape))

    def arrive(n, dst):
        pltpu.make_async_remote_copy(
            src_ref=dst, dst_ref=dst, send_sem=send_sems.at[n], recv_sem=recv_sems.at[n],
            device_id=(sibling, own), device_id_type=MESH,
        ).wait_recv()

    def features(part_of):
        return slice(part_of * SLICE, (part_of + 1) * SLICE)

    def block(r, part_of, tokens):
        return a_all.at[part_of, tokens, pl.ds(pl.multiple_of(r * SLICE, SLICE), SLICE)]

    def slab(at_x, part_of, tokens):
        return a_all.at[part_of, tokens, pl.ds(pl.multiple_of(at_x * 2 * SLICE, 2 * SLICE), 2 * SLICE)]

    def half_of(tokens, half):
        return pl.ds(pl.multiple_of(tokens.start + half * HALF, HALF), HALF)

    load_act = []
    for part_of in range(SLICES):
        load = pltpu.make_async_copy(act.at[:, features(part_of)], block(own, part_of, my_tokens), local_sems.at[4 + part_of])
        load.start()
        load_act.append(load)
    load_b = []
    for ch in range(2):
        load = pltpu.make_async_copy(
            grads.at[:, pl.ds(pl.multiple_of((2 * ch + core) * BS, BS), BS)],
            b_all.at[ch, pl.ds(pl.multiple_of(core * BS, BS), BS), :],
            local_sems.at[1 + ch],
        )
        load.start()
        load_b.append(load)
    load_stale = pltpu.make_async_copy(stale, stale_v, local_sems.at[3])
    load_stale.start()

    barrier = pltpu.get_barrier_semaphore()
    partners = [(dp, own_at(i)) for i in range(1, 8)]
    partners += [(dp_at(i), own) for i in range(1, N_DP)]
    for partner in partners:
        pl.semaphore_signal(barrier, inc=1, device_id=partner, device_id_type=MESH)

    flag[...] = jnp.full((8, 128), moved[0, 0].astype(F32))

    pl.semaphore_wait(barrier, len(partners))

    n_flag = new_sem()
    n_b = [new_sem() for _ in range(2)]
    n_own = [new_sem() for _ in range(SLICES)]
    n_pair = [new_sem() for _ in range(SLICES)]
    next_dp = lax.rem(dp + 1, N_DP)
    for ch in range(2):
        send(
            n_b[ch],
            grads.at[:, pl.ds(pl.multiple_of((2 * ch + 1 - core) * BS, BS), BS)],
            b_all.at[ch, my_tokens, :],
            sibling, own,
        )
    n_first_up, n_first_down = new_sem(), new_sem()
    for part_of in range(SLICES):
        target = block(own, part_of, my_tokens)
        send(n_pair[part_of], act.at[:, features(part_of)], target, dp, pair)
        send(n_own[part_of], act.at[:, features(part_of)], target, sibling, own)
        if part_of == 0:
            send(n_first_up, act.at[:, features(0)], target, dp, x_plus)
            send(n_first_down, act.at[:, features(0)], target, dp, x_minus)
    send(n_flag, flag, flag_prev, next_dp, own)

    def products_here(r, part_of):
        for ch in range(2):
            target = lax.rem(lax.rem(r, 2) * 2 + ch - y + 4, 4)
            lanes = pl.ds(pl.multiple_of(r * SLICE, SLICE), SLICE)
            value = dot(a_all[part_of, :, lanes], b_all[ch], (0, 0)) * (1.0 / TOKENS)
            part[0, target, features(part_of), :] = value.astype(BF16)

    def products(part_of, first, last):
        rows = features(part_of)
        for ch in range(2):
            @pl.loop(first, last)
            def _(slot):
                at_x = lax.rem(x + slot + slot // 2 - 2 * (slot // 3), 4)
                lanes = pl.ds(pl.multiple_of(at_x * 2 * SLICE, 2 * SLICE), 2 * SLICE)
                value = dot(a_all[part_of, :, lanes], b_all[ch], (0, 0)) * (1.0 / TOKENS)
                value = value.astype(BF16)
                for parity in range(2):
                    target = lax.rem(2 * parity + ch - y + 4, 4)
                    part[slot, target, rows, :] = value[parity * SLICE:(parity + 1) * SLICE]

    for load in load_act + load_b:
        load.wait()
    for ch in range(2):
        arrive(n_b[ch], b_all.at[ch, sib_tokens, :])
    y_sems = [[new_sem() for _ in range(6)] for _ in Y_PIECES]
    z_sems = [[new_sem() for _ in range(6)] for _ in Z_PIECES]
    grad_sems = [new_sem() for _ in Z_PIECES]
    y_up, y_down = (dp_y(1), own), (dp_y(3), own)
    z_up, z_down = (dp_z(1), own), (dp_z(3), own)

    def cut(first, rows):
        middle = first + rows // 2
        return slice(first, middle), slice(middle, first + rows)

    in_first = [lax.rem(y + by, 4) // 2 == z_lo for by in range(4)]

    def y_far(piece, keep=True):
        start, stop, row, rows = Y_PIECES[piece]
        lo, hi = cut(row, rows)
        sems = y_sems[piece]
        send(sems[0], part.at[start:stop, 2, lo], y_relay.at[start:stop, lo], *y_up, keep=keep)
        send(sems[1], part.at[start:stop, 2, hi], y_relay.at[start:stop, hi], *y_down, keep=keep)

    def y_near(piece, by, keep=True):
        start, stop, row, rows = Y_PIECES[piece]
        lo, hi = cut(row, rows)
        sems = y_sems[piece]
        if by == 1:
            send(sems[2], part.at[start:stop, 1, hi], y_from_minus.at[start:stop, hi], *y_up, keep=keep)
        else:
            send(sems[3], part.at[start:stop, 3, lo], y_from_plus.at[start:stop, lo], *y_down, keep=keep)

    def y_dir(piece):
        y_near(piece, 1)
        y_near(piece, 3)

    def y_relayed(piece, by, keep=True):
        start, stop, row, rows = Y_PIECES[piece]
        lo, hi = cut(row, rows)
        slots = slice(start, stop)
        sems = y_sems[piece]
        rows, n, to, target = (lo, 0, y_up, y_from_minus) if by == 1 else (hi, 1, y_down, y_from_plus)
        arrive(sems[n], y_relay.at[slots, rows])
        y_sum[slots, rows] = part[slots, by, rows] + y_relay[slots, rows]
        send(sems[4 + n], y_sum.at[slots, rows], target.at[slots, rows], *to, keep=keep)

    def y_b(piece):
        y_relayed(piece, 1)
        y_relayed(piece, 3)

    def y_a_step(piece, first):
        pl.when(in_first[2] == first)(functools.partial(y_far, piece, first))
        for by in (1, 3):
            pl.when(in_first[by] == first)(functools.partial(y_near, piece, by, first))

    def y_b_step(piece, first):
        for by in (1, 3):
            pl.when(in_first[by] == first)(functools.partial(y_relayed, piece, by, first))

    def y_c(piece):
        start, stop, row, rows = Y_PIECES[piece]
        slots = slice(start, stop)
        lo, hi = cut(row, rows)
        sems = y_sems[piece]
        arrive(sems[2], y_from_minus.at[slots, hi])
        arrive(sems[3], y_from_plus.at[slots, lo])
        arrive(sems[4], y_from_minus.at[slots, lo])
        arrive(sems[5], y_from_plus.at[slots, hi])
        every = slice(row, row + rows)
        for slot in range(start, stop):
            total = part[slot, 0, every].astype(F32) + y_from_minus[slot, every].astype(F32)
            total = total + y_from_plus[slot, every].astype(F32)
            ysum[lax.rem(x + X_ORDER[slot] - z + 4, 4), every] = total.astype(BF16)

    def z_far(piece):
        lo, hi = cut(*Z_PIECES[piece])
        sems = z_sems[piece]
        send(sems[0], ysum.at[2, lo], z_relay.at[lo], *z_up)
        send(sems[1], ysum.at[2, hi], z_relay.at[hi], *z_down)

    def z_dir(piece):
        lo, hi = cut(*Z_PIECES[piece])
        sems = z_sems[piece]
        send(sems[2], ysum.at[1, hi], z_from_minus.at[hi], *z_up)
        send(sems[3], ysum.at[3, lo], z_from_plus.at[lo], *z_down)

    def z_b(piece):
        lo, hi = cut(*Z_PIECES[piece])
        sems = z_sems[piece]
        arrive(sems[0], z_relay.at[lo])
        z_sum[lo] = ysum[1, lo] + z_relay[lo]
        send(sems[4], z_sum.at[lo], z_from_minus.at[lo], *z_up)
        arrive(sems[1], z_relay.at[hi])
        z_sum[hi] = ysum[3, hi] + z_relay[hi]
        send(sems[5], z_sum.at[hi], z_from_plus.at[hi], *z_down)

    def z_c(piece):
        row, rows = Z_PIECES[piece]
        lo, hi = cut(row, rows)
        sems = z_sems[piece]
        arrive(sems[2], z_from_minus.at[hi])
        arrive(sems[3], z_from_plus.at[lo])
        arrive(sems[4], z_from_minus.at[lo])
        arrive(sems[5], z_from_plus.at[hi])
        every = slice(row, row + rows)
        total = ysum[0, every].astype(F32) + z_from_minus[every].astype(F32)
        total = total + z_from_plus[every].astype(F32)
        grad[every] = total.astype(BF16)

    def shift(piece):
        row, rows = Z_PIECES[piece]
        every = slice(row, row + rows)
        send(grad_sems[piece], grad.at[every], grad_prev.at[every], next_dp, own)

    x_next, x_prev, x_far = lax.rem(x + 1, 4), lax.rem(x + 3, 4), lax.rem(x + 2, 4)
    n_up = [new_sem() for _ in range(SLICES)]
    n_down = [new_sem() for _ in range(SLICES)]
    n_far = [[new_sem(), new_sem()] for _ in range(SLICES)]

    def give(src, to_dp, to_own):
        n = new_sem()
        send(n, src, src, to_dp, to_own)
        return n

    n_sib_pair, n_sib = {}, [[] for _ in range(SLICES)]

    def take_pair(part_of):
        arrive(n_pair[part_of], block(pair, part_of, my_tokens))
        n_sib_pair[part_of] = give(block(pair, part_of, my_tokens), sibling, own)

    def along_x(part_of):
        mine = block(pair, 0, my_tokens) if part_of == 0 else slab(x, part_of, my_tokens)
        send(n_up[part_of], mine, mine, dp, x_plus)
        send(n_down[part_of], mine, mine, dp, x_minus)

    def take_near(part_of):
        if part_of == 0:
            arrive(n_first_up, block(x_minus, 0, my_tokens))
            arrive(n_first_down, block(x_plus, 0, my_tokens))
        for n, at_x, half, to in ((n_up, x_prev, 0, x_plus), (n_down, x_next, 1, x_minus)):
            if part_of == 0:
                arrive(n[0], block(lax.rem(at_x * 2 + 1 - z_lo, N_OWN), 0, my_tokens))
            else:
                arrive(n[part_of], slab(at_x, part_of, my_tokens))
            onward = slab(at_x, part_of, half_of(my_tokens, half))
            send(n_far[part_of][half], onward, onward, dp, to)
            n_sib[part_of].append((give(slab(at_x, part_of, my_tokens), sibling, own), slab(at_x, part_of, sib_tokens)))

    def take_far(part_of):
        for half in range(2):
            arrive(n_far[part_of][half], slab(x_far, part_of, half_of(my_tokens, half)))
            n = give(slab(x_far, part_of, half_of(my_tokens, half)), sibling, own)
            n_sib[part_of].append((n, slab(x_far, part_of, half_of(sib_tokens, half))))

    def prod_own(part_of):
        arrive(n_own[part_of], block(own, part_of, sib_tokens))
        products_here(own, part_of)

    def prod_pair(part_of):
        arrive(n_sib_pair[part_of], block(pair, part_of, sib_tokens))
        products_here(pair, part_of)

    def prod_near(part_of):
        for n, ref in n_sib[part_of][:2]:
            arrive(n, ref)
        products(part_of, 1, 3)

    def prod_far(part_of):
        for n, ref in n_sib[part_of][2:]:
            arrive(n, ref)
        products(part_of, 3, 4)

    prod_own(0)
    y_a_step(0, True)
    prod_own(1)
    take_pair(0)
    y_a_step(1, True)
    along_x(0)
    prod_pair(0)
    y_a_step(0, False)
    prod_own(2)
    take_pair(1)
    along_x(1)
    y_a_step(2, True)
    prod_pair(1)
    y_a_step(1, False)
    take_pair(2)
    y_b_step(1, True)
    y_b_step(0, False)
    prod_own(3)
    take_near(0)
    prod_pair(2)
    y_b_step(0, True)
    y_a_step(2, False)
    y_a_step(3, True)
    prod_near(0)
    along_x(2)
    y_dir(4)
    take_near(1)
    y_b_step(1, False)
    y_far(4)
    y_c(0)
    take_far(0)
    y_b_step(2, True)
    prod_near(1)
    prod_far(0)
    take_pair(3)
    along_x(3)
    y_dir(5)
    y_far(5)
    take_near(2)
    y_b(4)
    prod_pair(3)
    take_far(1)
    prod_near(2)
    y_a_step(3, False)
    prod_far(1)
    y_b(5)
    y_far(7)
    y_dir(7)
    y_c(4)
    y_b_step(3, True)
    y_c(5)
    take_far(2)
    take_near(3)
    y_far(6)
    prod_far(2)
    y_b_step(2, False)
    y_far(9)
    prod_near(3)
    z_far(0)
    z_far(1)
    y_b(7)
    take_far(3)
    prod_far(3)
    y_dir(6)
    y_b(6)
    y_b_step(3, False)
    y_b(9)
    y_c(1)
    y_c(7)
    z_dir(0)
    y_dir(9)
    z_far(3)
    z_b(1)
    y_far(10)
    z_dir(1)
    y_far(8)
    z_b(0)
    y_c(2)
    z_dir(3)
    y_c(6)
    z_far(2)
    z_b(3)
    y_far(11)
    y_c(9)
    z_far(5)
    z_dir(5)
    y_c(3)
    y_dir(10)
    y_b(10)
    z_c(0)
    z_dir(2)
    y_b(11)
    y_dir(11)
    y_b(8)
    y_dir(8)
    z_b(5)
    z_b(2)
    y_c(10)
    z_far(6)
    z_dir(6)
    shift(0)
    y_c(11)
    z_dir(7)
    z_far(7)
    z_c(5)
    z_b(6)
    y_c(8)
    z_far(4)
    z_b(7)
    z_dir(4)
    z_c(3)
    z_c(1)
    z_b(4)
    z_c(6)
    shift(1)
    z_c(2)
    shift(3)
    shift(5)
    z_c(7)
    shift(7)
    shift(6)
    shift(2)
    z_c(4)
    shift(4)

    load_stale.wait()
    squares = jnp.zeros((1, 1), F32)
    for half in range(2):
        rows = slice(half * HALF, (half + 1) * HALF)
        left_applied[rows, :] = dot(stale_v[0, 0, rows, :], grad[...]).astype(BF16)
        value = dot(left_applied[rows, :], stale_v[0, 1])
        precond[rows, :] = value
        squares = squares + jnp.sum(value * value, keepdims=True)
    keep_precond = pltpu.make_async_copy(precond, precond_out, local_sems.at[0])
    keep_precond.start()

    def spread(store, value, targets):
        store[0] = jnp.broadcast_to(value, (8, 128))
        sems = [new_sem() for _ in targets]
        for i, target in enumerate(targets):
            send(sems[i], store.at[0], store.at[i + 1], *target)
        return sems

    def collect(store, sems):
        for i, n in enumerate(sems):
            arrive(n, store.at[i + 1])
        return jnp.sum(store[...], axis=0)[0:1, 0:1]

    def root(tile, side, slot, keep):
        total = jnp.zeros((1, 1), F32)
        for half in range(2):
            rows = slice(half * HALF, (half + 1) * HALF)
            if side == 0:
                value = dot(tile[rows, :], tile[...], (1, 1))
            else:
                value = dot(tile[:, rows], tile[...], (0, 0))
            value = value + EPSILON * identity_rows(half * HALF, HALF)
            stat[rows, :] = value
            total = total + jnp.sum(value * value, keepdims=True)
        scale = 2.5 / jnp.sqrt(total)
        matrix = stat[...] * scale
        stat[...] = matrix
        stat_b[...] = matrix.astype(BF16)
        for half in range(2):
            rows = slice(half * HALF, (half + 1) * HALF)
            squared = dot(stat_b[rows, :], stat_b[...])
            matrix = stat[rows, :]
            mid_n[rows, :] = (5.0 * matrix - squared) * 0.25
            mid_e[rows, :] = ((squared - 10.0 * matrix) * 0.0625).astype(BF16)
        for half in range(2):
            rows = slice(half * HALF, (half + 1) * HALF)
            value = 1.5625 * mid_n[rows, :] + dot(mid_e[rows, :], mid_n[...].astype(BF16))
            mid_t[rows, :] = value
            mid_tb[rows, :] = value.astype(BF16)
        factor = jnp.sqrt(jnp.sqrt(scale)) * 0.25
        for half in range(2):
            rows = slice(half * HALF, (half + 1) * HALF)
            value = 1.5625 * mid_t[rows, :] + dot(mid_e[rows, :], mid_tb[...])
            first = (25.0 * identity_rows(half * HALF, HALF) - 5.0 * stat[rows, :]) * 0.25
            result = ((first - value) * factor).astype(BF16)
            fresh[slot, side, rows, :] = (result.astype(F32) * keep).astype(BF16)

    keep_fresh = []

    def keep_root(slot, side):
        copy = pltpu.make_async_copy(fresh.at[slot, side], fresh_out.at[slot, side], local_sems.at[4 + 2 * slot + side])
        copy.start()
        keep_fresh.append(copy)

    sems1 = spread(norm1, squares, [(dp, own_at(i)) for i in range(1, N_OWN)])
    keep = 1.0 - flag[0:1, 0:1]
    root(grad, 0, 0, keep)
    keep_root(0, 0)
    sems2 = spread(norm2, collect(norm1, sems1), [(dp_at(i), own) for i in range(1, N_DP)])
    root(grad, 1, 0, keep)
    keep_root(0, 1)
    arrive(n_flag, flag_prev)
    for n, (row, rows) in zip(grad_sems, Z_PIECES):
        arrive(n, grad_prev.at[row:row + rows])
    keep = flag_prev[0:1, 0:1]
    for side in range(2):
        root(grad_prev, side, 1, keep)
        keep_root(1, side)
    norm_out[...] = jnp.broadcast_to(collect(norm2, sems2), (8, 128))

    for copy in keep_fresh:
        copy.wait()
    keep_precond.wait()
    for n, shape in sent:
        if shape[0] == 8:
            ref = norm1.at[0]
        elif len(shape) == 2:
            ref = part.at[0, 0, 0:shape[0], 0:shape[1]]
        else:
            ref = part.at[0:shape[0], 0, 0:shape[1]]
        pltpu.make_async_remote_copy(
            src_ref=ref, dst_ref=ref, send_sem=send_sems.at[n], recv_sem=recv_sems.at[n],
            device_id=(sibling, own), device_id_type=MESH,
        ).wait_send()
    assert counter[0] <= N_SEMS, counter[0]


def finish(precond, fresh, norm, update, fresh_out, value, result, roots, sems):
    tiles = [(slot, side) for slot in range(2) for side in range(2)]
    load = pltpu.make_async_copy(precond, value, sems.at[0])
    loads = [pltpu.make_async_copy(fresh.at[t], roots.at[t], sems.at[2 + i]) for i, t in enumerate(tiles)]
    stores = [pltpu.make_async_copy(roots.at[t], fresh_out.at[t], sems.at[6 + i]) for i, t in enumerate(tiles)]
    store = pltpu.make_async_copy(result, update, sems.at[1])
    load.start()
    for copy in loads:
        copy.start()
    scale = lax.rsqrt(norm[0:1, 0:1] / ENTRIES + 1e-06)
    load.wait()
    result[0] = (value[...] * scale).astype(BF16)
    store.start()
    for arrived, leave in zip(loads, stores):
        arrived.wait()
        leave.start()
    for copy in stores + [store]:
        copy.wait()


def body(activations, out_grads, moved_tiles, stale_roots):
    tile = (BS, BS)
    scratch = [
        ((SLICES, 2 * BS, N_OWN * SLICE), BF16),
        ((2, 2 * BS, BS), BF16),
        ((4, 4) + tile, BF16),
        ((4,) + tile, BF16), ((4,) + tile, BF16), ((4,) + tile, BF16), ((4,) + tile, BF16),
        ((4,) + tile, BF16),
        (tile, BF16), (tile, BF16), (tile, BF16), (tile, BF16),
        (tile, BF16), (tile, BF16), ((8, 128), F32), ((8, 128), F32), ((1, 2) + tile, BF16),
        (tile, BF16), (tile, F32), (tile, F32), (tile, BF16), (tile, F32), (tile, BF16),
        (tile, F32), (tile, BF16),
        ((N_OWN, 8, 128), F32), ((N_DP, 8, 128), F32), ((2, 2) + tile, BF16),
    ]
    flops = 2 * 2 * 512 * 4096 * 2048
    precond, fresh, norm = pl.pallas_call(
        kernel,
        out_shape=(
            jax.ShapeDtypeStruct(tile, F32),
            jax.ShapeDtypeStruct((2, 2) + tile, BF16),
            jax.ShapeDtypeStruct((8, 128), F32),
        ),
        in_specs=[
            pl.BlockSpec(memory_space=pl.ANY),
            pl.BlockSpec(memory_space=pl.ANY),
            pl.BlockSpec(memory_space=pltpu.SMEM),
            pl.BlockSpec(memory_space=pl.ANY),
        ],
        out_specs=(
            pl.BlockSpec(memory_space=pl.ANY),
            pl.BlockSpec(memory_space=pl.ANY),
            pl.BlockSpec(memory_space=pltpu.VMEM),
        ),
        scratch_shapes=[pltpu.VMEM(shape, dtype) for shape, dtype in scratch] + [
            pltpu.SemaphoreType.DMA((N_SEMS,)),
            pltpu.SemaphoreType.DMA((N_SEMS,)),
            pltpu.SemaphoreType.DMA((4 + SLICES,)),
        ],
        compiler_params=pltpu.CompilerParams(
            collective_id=0, has_side_effects=True, vmem_limit_bytes=60 * 1024 * 1024
        ),
        cost_estimate=pl.CostEstimate(flops=flops, bytes_accessed=6 << 20, transcendentals=0),
    )(activations, out_grads, moved_tiles, stale_roots)
    return tuple(pl.pallas_call(
        finish,
        out_shape=(
            jax.ShapeDtypeStruct((1,) + tile, BF16),
            jax.ShapeDtypeStruct((2, 2) + tile, BF16),
        ),
        in_specs=[
            pl.BlockSpec(memory_space=pl.ANY),
            pl.BlockSpec(memory_space=pl.ANY),
            pl.BlockSpec(memory_space=pltpu.VMEM),
        ],
        out_specs=(pl.BlockSpec(memory_space=pl.ANY), pl.BlockSpec(memory_space=pl.ANY)),
        scratch_shapes=[
            pltpu.VMEM(tile, F32),
            pltpu.VMEM((1,) + tile, BF16),
            pltpu.VMEM((2, 2) + tile, BF16),
            pltpu.SemaphoreType.DMA((10,)),
        ],
    )(precond, fresh, norm))


def solution(mesh):
    in_specs = (P("dp", "own"), P("dp", "own"), P("dp", "own"), P("dp", None, None, "own"))
    out_specs = (P("dp", None, "own"), P("dp", None, None, "own"))
    return jax.shard_map(body, mesh=mesh, in_specs=in_specs, out_specs=out_specs, check_vma=False)
```

```python
import functools

import jax
import jax.numpy as jnp
from jax import lax
from jax.experimental import pallas as pl
from jax.experimental.pallas import tpu as pltpu
from jax.sharding import PartitionSpec as P

N_DP = 32
N_OWN = 8
BS = 512
HALF = BS // 2
TOKENS = 16384
EPSILON = 1e-06
ENTRIES = N_DP * N_OWN * BS * BS

MESH = pl.DeviceIdType.MESH
F32 = jnp.float32
BF16 = jnp.bfloat16

X_ORDER = (0, 1, 3, 2)
SLICE = 128
SLICES = BS // SLICE
Y_PIECES = (
    (0, 1, 0, 128), (0, 1, 128, 128), (0, 1, 256, 128), (0, 1, 384, 128), (1, 3, 0, 128),
    (3, 4, 0, 128), (1, 4, 128, 64), (1, 4, 192, 64), (1, 4, 256, 64), (1, 4, 320, 64),
    (1, 4, 384, 64), (1, 4, 448, 64),
)
Z_PIECES = ((0, 64), (64, 64), (128, 64), (192, 64), (256, 64), (320, 64), (384, 64), (448, 64))

N_SEMS = 320


def dot(left, right, contract=(1, 0)):
    dims = (((contract[0],), (contract[1],)), ((), ()))
    return lax.dot_general(left, right, dims, preferred_element_type=F32)


def identity_rows(first_row, rows):
    row = lax.broadcasted_iota(jnp.int32, (rows, BS), 0) + first_row
    column = lax.broadcasted_iota(jnp.int32, (rows, BS), 1)
    return (row == column).astype(F32)


def kernel(
    act, grads, moved, stale,
    precond_out, fresh_out, norm_out,
    a_all, b_all, part,
    y_relay, y_sum, y_from_minus, y_from_plus,
    ysum,
    z_relay, z_sum, z_from_minus, z_from_plus,
    grad, grad_prev, flag, flag_prev, stale_v,
    left_applied, precond, stat, stat_b, mid_n, mid_e, mid_t, mid_tb,
    norm1, norm2, fresh,
    send_sems, recv_sems, local_sems,
):
    dp = lax.axis_index("dp")
    own = lax.axis_index("own")
    core = lax.rem(dp, 2)
    y = lax.rem(dp // 2, 4)
    z = dp // 8
    x = own // 2
    z_lo = lax.rem(own, 2)

    sibling = dp + 1 - 2 * core
    pair = own + 1 - 2 * z_lo
    x_plus, x_minus = lax.rem(own + 2, N_OWN), lax.rem(own + 6, N_OWN)

    def dp_y(by):
        return z * 8 + lax.rem(y + by, 4) * 2 + core

    def dp_at(by):
        return lax.rem(dp + by, N_DP)

    def dp_z(by):
        return dp_at(8 * by)

    def own_at(by):
        return lax.rem(own + by, N_OWN)

    sent = []
    counter = [0]
    my_tokens = pl.ds(pl.multiple_of(core * BS, BS), BS)
    sib_tokens = pl.ds(pl.multiple_of((1 - core) * BS, BS), BS)

    def new_sem():
        counter[0] += 1
        return counter[0] - 1

    def send(n, src, dst, to_dp, to_own, keep=True):
        copy = pltpu.make_async_remote_copy(
            src_ref=src, dst_ref=dst, send_sem=send_sems.at[n], recv_sem=recv_sems.at[n],
            device_id=(to_dp, to_own), device_id_type=MESH,
        )
        copy.start()
        if keep:
            sent.append((n, src.shape))

    def arrive(n, dst):
        pltpu.make_async_remote_copy(
            src_ref=dst, dst_ref=dst, send_sem=send_sems.at[n], recv_sem=recv_sems.at[n],
            device_id=(sibling, own), device_id_type=MESH,
        ).wait_recv()

    def features(part_of):
        return slice(part_of * SLICE, (part_of + 1) * SLICE)

    def block(r, part_of, tokens):
        return a_all.at[part_of, tokens, pl.ds(pl.multiple_of(r * SLICE, SLICE), SLICE)]

    def slab(at_x, part_of, tokens):
        return a_all.at[part_of, tokens, pl.ds(pl.multiple_of(at_x * 2 * SLICE, 2 * SLICE), 2 * SLICE)]

    def half_of(tokens, half):
        return pl.ds(pl.multiple_of(tokens.start + half * HALF, HALF), HALF)

    load_act = []
    for part_of in range(SLICES):
        load = pltpu.make_async_copy(act.at[:, features(part_of)], block(own, part_of, my_tokens), local_sems.at[4 + part_of])
        load.start()
        load_act.append(load)
    load_b = []
    for ch in range(2):
        load = pltpu.make_async_copy(
            grads.at[:, pl.ds(pl.multiple_of((2 * ch + core) * BS, BS), BS)],
            b_all.at[ch, pl.ds(pl.multiple_of(core * BS, BS), BS), :],
            local_sems.at[1 + ch],
        )
        load.start()
        load_b.append(load)
    load_stale = pltpu.make_async_copy(stale, stale_v, local_sems.at[3])
    load_stale.start()

    cross = lax.rem(dp + 2 * core - 1 + N_DP, N_DP)
    barrier = pltpu.get_barrier_semaphore()
    partners = [(dp, own_at(i)) for i in range(1, 8)]
    partners += [(sibling, own_at(i)) for i in range(N_OWN)]
    partners += [(dp_at(2 * i), own) for i in range(1, N_DP // 2)]
    partners += [(cross, own)]
    for partner in partners:
        pl.semaphore_signal(barrier, inc=1, device_id=partner, device_id_type=MESH)

    flag[...] = jnp.full((8, 128), moved[0, 0].astype(F32))

    pl.semaphore_wait(barrier, len(partners))

    n_flag = new_sem()
    n_b = [new_sem() for _ in range(2)]
    n_own = [new_sem() for _ in range(SLICES)]
    n_pair = [new_sem() for _ in range(SLICES)]
    next_dp = lax.rem(dp + 1, N_DP)
    for ch in range(2):
        send(
            n_b[ch],
            grads.at[:, pl.ds(pl.multiple_of((2 * ch + 1 - core) * BS, BS), BS)],
            b_all.at[ch, my_tokens, :],
            sibling, own,
        )
    n_first_up, n_first_down = new_sem(), new_sem()
    for part_of in range(SLICES):
        target = block(own, part_of, my_tokens)
        send(n_pair[part_of], act.at[:, features(part_of)], target, dp, pair)
        send(n_own[part_of], act.at[:, features(part_of)], target, sibling, own)
        if part_of == 0:
            send(n_first_up, act.at[:, features(0)], target, dp, x_plus)
            send(n_first_down, act.at[:, features(0)], target, dp, x_minus)
    send(n_flag, flag, flag_prev, next_dp, own)

    def products_here(r, part_of):
        for ch in range(2):
            target = lax.rem(lax.rem(r, 2) * 2 + ch - y + 4, 4)
            lanes = pl.ds(pl.multiple_of(r * SLICE, SLICE), SLICE)
            value = dot(a_all[part_of, :, lanes], b_all[ch], (0, 0)) * (1.0 / TOKENS)
            part[0, target, features(part_of), :] = value.astype(BF16)

    def products(part_of, first, last):
        rows = features(part_of)
        for ch in range(2):
            @pl.loop(first, last)
            def _(slot):
                at_x = lax.rem(x + slot + slot // 2 - 2 * (slot // 3), 4)
                lanes = pl.ds(pl.multiple_of(at_x * 2 * SLICE, 2 * SLICE), 2 * SLICE)
                value = dot(a_all[part_of, :, lanes], b_all[ch], (0, 0)) * (1.0 / TOKENS)
                value = value.astype(BF16)
                for parity in range(2):
                    target = lax.rem(2 * parity + ch - y + 4, 4)
                    part[slot, target, rows, :] = value[parity * SLICE:(parity + 1) * SLICE]

    for load in load_act + load_b:
        load.wait()
    for ch in range(2):
        arrive(n_b[ch], b_all.at[ch, sib_tokens, :])
    y_sems = [[new_sem() for _ in range(6)] for _ in Y_PIECES]
    z_sems = [[new_sem() for _ in range(6)] for _ in Z_PIECES]
    grad_sems = [new_sem() for _ in Z_PIECES]
    y_up, y_down = (dp_y(1), own), (dp_y(3), own)
    z_up, z_down = (dp_z(1), own), (dp_z(3), own)

    def cut(first, rows):
        middle = first + rows // 2
        return slice(first, middle), slice(middle, first + rows)

    in_first = [lax.rem(y + by, 4) // 2 == z_lo for by in range(4)]

    def y_far(piece, keep=True):
        start, stop, row, rows = Y_PIECES[piece]
        lo, hi = cut(row, rows)
        sems = y_sems[piece]
        send(sems[0], part.at[start:stop, 2, lo], y_relay.at[start:stop, lo], *y_up, keep=keep)
        send(sems[1], part.at[start:stop, 2, hi], y_relay.at[start:stop, hi], *y_down, keep=keep)

    def y_near(piece, by, keep=True):
        start, stop, row, rows = Y_PIECES[piece]
        lo, hi = cut(row, rows)
        sems = y_sems[piece]
        if by == 1:
            send(sems[2], part.at[start:stop, 1, hi], y_from_minus.at[start:stop, hi], *y_up, keep=keep)
        else:
            send(sems[3], part.at[start:stop, 3, lo], y_from_plus.at[start:stop, lo], *y_down, keep=keep)

    def y_dir(piece):
        y_near(piece, 1)
        y_near(piece, 3)

    def y_relayed(piece, by, keep=True):
        start, stop, row, rows = Y_PIECES[piece]
        lo, hi = cut(row, rows)
        slots = slice(start, stop)
        sems = y_sems[piece]
        rows, n, to, target = (lo, 0, y_up, y_from_minus) if by == 1 else (hi, 1, y_down, y_from_plus)
        arrive(sems[n], y_relay.at[slots, rows])
        y_sum[slots, rows] = part[slots, by, rows] + y_relay[slots, rows]
        send(sems[4 + n], y_sum.at[slots, rows], target.at[slots, rows], *to, keep=keep)

    def y_b(piece):
        y_relayed(piece, 1)
        y_relayed(piece, 3)

    def y_a_step(piece, first):
        pl.when(in_first[2] == first)(functools.partial(y_far, piece, first))
        for by in (1, 3):
            pl.when(in_first[by] == first)(functools.partial(y_near, piece, by, first))

    def y_b_step(piece, first):
        for by in (1, 3):
            pl.when(in_first[by] == first)(functools.partial(y_relayed, piece, by, first))

    def y_c(piece):
        start, stop, row, rows = Y_PIECES[piece]
        slots = slice(start, stop)
        lo, hi = cut(row, rows)
        sems = y_sems[piece]
        arrive(sems[2], y_from_minus.at[slots, hi])
        arrive(sems[3], y_from_plus.at[slots, lo])
        arrive(sems[4], y_from_minus.at[slots, lo])
        arrive(sems[5], y_from_plus.at[slots, hi])
        every = slice(row, row + rows)
        for slot in range(start, stop):
            total = part[slot, 0, every].astype(F32) + y_from_minus[slot, every].astype(F32)
            total = total + y_from_plus[slot, every].astype(F32)
            ysum[lax.rem(x + X_ORDER[slot] - z + 4, 4), every] = total.astype(BF16)

    def z_far(piece):
        lo, hi = cut(*Z_PIECES[piece])
        sems = z_sems[piece]
        send(sems[0], ysum.at[2, lo], z_relay.at[lo], *z_up)
        send(sems[1], ysum.at[2, hi], z_relay.at[hi], *z_down)

    def z_dir(piece):
        lo, hi = cut(*Z_PIECES[piece])
        sems = z_sems[piece]
        send(sems[2], ysum.at[1, hi], z_from_minus.at[hi], *z_up)
        send(sems[3], ysum.at[3, lo], z_from_plus.at[lo], *z_down)

    def z_b(piece):
        lo, hi = cut(*Z_PIECES[piece])
        sems = z_sems[piece]
        arrive(sems[0], z_relay.at[lo])
        z_sum[lo] = ysum[1, lo] + z_relay[lo]
        send(sems[4], z_sum.at[lo], z_from_minus.at[lo], *z_up)
        arrive(sems[1], z_relay.at[hi])
        z_sum[hi] = ysum[3, hi] + z_relay[hi]
        send(sems[5], z_sum.at[hi], z_from_plus.at[hi], *z_down)

    def z_c(piece):
        row, rows = Z_PIECES[piece]
        lo, hi = cut(row, rows)
        sems = z_sems[piece]
        arrive(sems[2], z_from_minus.at[hi])
        arrive(sems[3], z_from_plus.at[lo])
        arrive(sems[4], z_from_minus.at[lo])
        arrive(sems[5], z_from_plus.at[hi])
        every = slice(row, row + rows)
        total = ysum[0, every].astype(F32) + z_from_minus[every].astype(F32)
        total = total + z_from_plus[every].astype(F32)
        grad[every] = total.astype(BF16)

    def shift(piece):
        row, rows = Z_PIECES[piece]
        every = slice(row, row + rows)
        send(grad_sems[piece], grad.at[every], grad_prev.at[every], next_dp, own)

    x_next, x_prev, x_far = lax.rem(x + 1, 4), lax.rem(x + 3, 4), lax.rem(x + 2, 4)
    n_up = [new_sem() for _ in range(SLICES)]
    n_down = [new_sem() for _ in range(SLICES)]
    n_far = [[new_sem(), new_sem()] for _ in range(SLICES)]

    def give(src, to_dp, to_own):
        n = new_sem()
        send(n, src, src, to_dp, to_own)
        return n

    n_sib_pair, n_sib = {}, [[] for _ in range(SLICES)]

    def take_pair(part_of):
        arrive(n_pair[part_of], block(pair, part_of, my_tokens))
        n_sib_pair[part_of] = give(block(pair, part_of, my_tokens), sibling, own)

    def along_x(part_of):
        mine = block(pair, 0, my_tokens) if part_of == 0 else slab(x, part_of, my_tokens)
        send(n_up[part_of], mine, mine, dp, x_plus)
        send(n_down[part_of], mine, mine, dp, x_minus)

    def take_near(part_of):
        if part_of == 0:
            arrive(n_first_up, block(x_minus, 0, my_tokens))
            arrive(n_first_down, block(x_plus, 0, my_tokens))
        for n, at_x, half, to in ((n_up, x_prev, 0, x_plus), (n_down, x_next, 1, x_minus)):
            if part_of == 0:
                arrive(n[0], block(lax.rem(at_x * 2 + 1 - z_lo, N_OWN), 0, my_tokens))
            else:
                arrive(n[part_of], slab(at_x, part_of, my_tokens))
            onward = slab(at_x, part_of, half_of(my_tokens, half))
            send(n_far[part_of][half], onward, onward, dp, to)
            n_sib[part_of].append((give(slab(at_x, part_of, my_tokens), sibling, own), slab(at_x, part_of, sib_tokens)))

    def take_far(part_of):
        for half in range(2):
            arrive(n_far[part_of][half], slab(x_far, part_of, half_of(my_tokens, half)))
            n = give(slab(x_far, part_of, half_of(my_tokens, half)), sibling, own)
            n_sib[part_of].append((n, slab(x_far, part_of, half_of(sib_tokens, half))))

    def prod_own(part_of):
        arrive(n_own[part_of], block(own, part_of, sib_tokens))
        products_here(own, part_of)

    def prod_pair(part_of):
        arrive(n_sib_pair[part_of], block(pair, part_of, sib_tokens))
        products_here(pair, part_of)

    def prod_near(part_of):
        for n, ref in n_sib[part_of][:2]:
            arrive(n, ref)
        products(part_of, 1, 3)

    def prod_far(part_of):
        for n, ref in n_sib[part_of][2:]:
            arrive(n, ref)
        products(part_of, 3, 4)

    prod_own(0)
    y_a_step(0, True)
    prod_own(1)
    take_pair(0)
    y_a_step(1, True)
    along_x(0)
    prod_pair(0)
    y_a_step(0, False)
    prod_own(2)
    take_pair(1)
    along_x(1)
    y_a_step(2, True)
    prod_pair(1)
    y_a_step(1, False)
    take_pair(2)
    y_b_step(1, True)
    y_b_step(0, False)
    prod_own(3)
    take_near(0)
    prod_pair(2)
    y_b_step(0, True)
    y_a_step(2, False)
    y_a_step(3, True)
    prod_near(0)
    along_x(2)
    y_dir(4)
    take_near(1)
    y_b_step(1, False)
    y_far(4)
    y_c(0)
    take_far(0)
    y_b_step(2, True)
    prod_near(1)
    prod_far(0)
    take_pair(3)
    along_x(3)
    y_dir(5)
    y_far(5)
    take_near(2)
    y_b(4)
    prod_pair(3)
    take_far(1)
    prod_near(2)
    y_a_step(3, False)
    prod_far(1)
    y_b(5)
    y_far(7)
    y_dir(7)
    y_c(4)
    y_b_step(3, True)
    y_c(5)
    take_far(2)
    take_near(3)
    y_far(6)
    prod_far(2)
    y_b_step(2, False)
    y_far(9)
    prod_near(3)
    z_far(0)
    z_far(1)
    y_b(7)
    take_far(3)
    prod_far(3)
    y_dir(6)
    y_b(6)
    y_b_step(3, False)
    y_b(9)
    y_c(1)
    y_c(7)
    z_dir(0)
    y_dir(9)
    z_far(3)
    z_b(1)
    y_far(10)
    z_dir(1)
    y_far(8)
    z_b(0)
    y_c(2)
    z_dir(3)
    y_c(6)
    z_far(2)
    z_b(3)
    y_far(11)
    y_c(9)
    z_far(5)
    z_dir(5)
    y_c(3)
    y_dir(10)
    y_b(10)
    z_c(0)
    z_dir(2)
    y_b(11)
    y_dir(11)
    y_b(8)
    y_dir(8)
    z_b(5)
    z_b(2)
    y_c(10)
    z_far(6)
    z_dir(6)
    shift(0)
    y_c(11)
    z_dir(7)
    z_far(7)
    z_c(5)
    z_b(6)
    y_c(8)
    z_far(4)
    z_b(7)
    z_dir(4)
    z_c(3)
    z_c(1)
    z_b(4)
    z_c(6)
    shift(1)
    z_c(2)
    shift(3)
    shift(5)
    z_c(7)
    shift(7)
    shift(6)
    shift(2)
    z_c(4)
    shift(4)

    load_stale.wait()
    squares = jnp.zeros((1, 1), F32)
    for half in range(2):
        rows = slice(half * HALF, (half + 1) * HALF)
        left_applied[rows, :] = dot(stale_v[0, 0, rows, :], grad[...]).astype(BF16)
        value = dot(left_applied[rows, :], stale_v[0, 1])
        precond[rows, :] = value
        squares = squares + jnp.sum(value * value, keepdims=True)
    keep_precond = pltpu.make_async_copy(precond, precond_out, local_sems.at[0])
    keep_precond.start()

    def spread(store, value, targets):
        store[0] = jnp.broadcast_to(value, (8, 128))
        sems = [new_sem() for _ in targets]
        for i, target in enumerate(targets):
            send(sems[i], store.at[0], store.at[i + 1], *target)
        return sems

    def collect(store, sems):
        for i, n in enumerate(sems):
            arrive(n, store.at[i + 1])
        return jnp.sum(store[...], axis=0)[0:1, 0:1]

    def root(tile, side, slot, keep):
        total = jnp.zeros((1, 1), F32)
        for half in range(2):
            rows = slice(half * HALF, (half + 1) * HALF)
            if side == 0:
                value = dot(tile[rows, :], tile[...], (1, 1))
            else:
                value = dot(tile[:, rows], tile[...], (0, 0))
            value = value + EPSILON * identity_rows(half * HALF, HALF)
            stat[rows, :] = value
            total = total + jnp.sum(value * value, keepdims=True)
        scale = 2.5 / jnp.sqrt(total)
        matrix = stat[...] * scale
        stat[...] = matrix
        stat_b[...] = matrix.astype(BF16)
        for half in range(2):
            rows = slice(half * HALF, (half + 1) * HALF)
            squared = dot(stat_b[rows, :], stat_b[...])
            matrix = stat[rows, :]
            mid_n[rows, :] = (5.0 * matrix - squared) * 0.25
            mid_e[rows, :] = ((squared - 10.0 * matrix) * 0.0625).astype(BF16)
        for half in range(2):
            rows = slice(half * HALF, (half + 1) * HALF)
            value = 1.5625 * mid_n[rows, :] + dot(mid_e[rows, :], mid_n[...].astype(BF16))
            mid_t[rows, :] = value
            mid_tb[rows, :] = value.astype(BF16)
        factor = jnp.sqrt(jnp.sqrt(scale)) * 0.25
        for half in range(2):
            rows = slice(half * HALF, (half + 1) * HALF)
            value = 1.5625 * mid_t[rows, :] + dot(mid_e[rows, :], mid_tb[...])
            first = (25.0 * identity_rows(half * HALF, HALF) - 5.0 * stat[rows, :]) * 0.25
            result = ((first - value) * factor).astype(BF16)
            fresh[slot, side, rows, :] = (result.astype(F32) * keep).astype(BF16)

    keep_fresh = []

    def keep_root(slot, side):
        copy = pltpu.make_async_copy(fresh.at[slot, side], fresh_out.at[slot, side], local_sems.at[4 + 2 * slot + side])
        copy.start()
        keep_fresh.append(copy)

    near = [(dp, own_at(i)) for i in range(1, N_OWN)] + [(sibling, own_at(i)) for i in range(N_OWN)]
    sems1 = spread(norm1, squares, near)
    keep = 1.0 - flag[0:1, 0:1]
    root(grad, 0, 0, keep)
    keep_root(0, 0)
    sems2 = spread(norm2, collect(norm1, sems1), [(dp_at(2 * i), own) for i in range(1, N_DP // 2)])
    root(grad, 1, 0, keep)
    keep_root(0, 1)
    arrive(n_flag, flag_prev)
    for n, (row, rows) in zip(grad_sems, Z_PIECES):
        arrive(n, grad_prev.at[row:row + rows])
    keep = flag_prev[0:1, 0:1]
    for side in range(2):
        root(grad_prev, side, 1, keep)
        keep_root(1, side)
    norm_out[...] = jnp.broadcast_to(collect(norm2, sems2), (8, 128))

    for copy in keep_fresh:
        copy.wait()
    keep_precond.wait()
    for n, shape in sent:
        if shape[0] == 8:
            ref = norm1.at[0]
        elif len(shape) == 2:
            ref = part.at[0, 0, 0:shape[0], 0:shape[1]]
        else:
            ref = part.at[0:shape[0], 0, 0:shape[1]]
        pltpu.make_async_remote_copy(
            src_ref=ref, dst_ref=ref, send_sem=send_sems.at[n], recv_sem=recv_sems.at[n],
            device_id=(sibling, own), device_id_type=MESH,
        ).wait_send()
    assert counter[0] <= N_SEMS, counter[0]


def finish(precond, fresh, norm, update, fresh_out, value, result, roots, sems):
    tiles = [(slot, side) for slot in range(2) for side in range(2)]
    halves = [slice(half * HALF, (half + 1) * HALF) for half in range(2)]
    loads = [pltpu.make_async_copy(fresh.at[t], roots.at[t], sems.at[i]) for i, t in enumerate(tiles)]
    stores = [pltpu.make_async_copy(roots.at[t], fresh_out.at[t], sems.at[4 + i]) for i, t in enumerate(tiles)]
    values = [pltpu.make_async_copy(precond.at[h], value.at[h], sems.at[8 + i]) for i, h in enumerate(halves)]
    results = [pltpu.make_async_copy(result.at[0, h], update.at[0, h], sems.at[10 + i]) for i, h in enumerate(halves)]
    for copy in loads + values:
        copy.start()
    scale = lax.rsqrt(norm[0:1, 0:1] / ENTRIES + 1e-06)
    for arrived, leave in zip(loads, stores):
        arrived.wait()
        leave.start()
    for rows, arrived, leave in zip(halves, values, results):
        arrived.wait()
        result[0, rows] = (value[rows] * scale).astype(BF16)
        leave.start()
    for copy in stores + results:
        copy.wait()


def body(activations, out_grads, moved_tiles, stale_roots):
    tile = (BS, BS)
    scratch = [
        ((SLICES, 2 * BS, N_OWN * SLICE), BF16),
        ((2, 2 * BS, BS), BF16),
        ((4, 4) + tile, BF16),
        ((4,) + tile, BF16), ((4,) + tile, BF16), ((4,) + tile, BF16), ((4,) + tile, BF16),
        ((4,) + tile, BF16),
        (tile, BF16), (tile, BF16), (tile, BF16), (tile, BF16),
        (tile, BF16), (tile, BF16), ((8, 128), F32), ((8, 128), F32), ((1, 2) + tile, BF16),
        (tile, BF16), (tile, F32), (tile, F32), (tile, BF16), (tile, F32), (tile, BF16),
        (tile, F32), (tile, BF16),
        ((2 * N_OWN, 8, 128), F32), ((N_DP // 2, 8, 128), F32), ((2, 2) + tile, BF16),
    ]
    flops = 2 * 2 * 512 * 4096 * 2048
    precond, fresh, norm = pl.pallas_call(
        kernel,
        out_shape=(
            jax.ShapeDtypeStruct(tile, F32),
            jax.ShapeDtypeStruct((2, 2) + tile, BF16),
            jax.ShapeDtypeStruct((8, 128), F32),
        ),
        in_specs=[
            pl.BlockSpec(memory_space=pl.ANY),
            pl.BlockSpec(memory_space=pl.ANY),
            pl.BlockSpec(memory_space=pltpu.SMEM),
            pl.BlockSpec(memory_space=pl.ANY),
        ],
        out_specs=(
            pl.BlockSpec(memory_space=pl.ANY),
            pl.BlockSpec(memory_space=pl.ANY),
            pl.BlockSpec(memory_space=pltpu.VMEM),
        ),
        scratch_shapes=[pltpu.VMEM(shape, dtype) for shape, dtype in scratch] + [
            pltpu.SemaphoreType.DMA((N_SEMS,)),
            pltpu.SemaphoreType.DMA((N_SEMS,)),
            pltpu.SemaphoreType.DMA((4 + SLICES,)),
        ],
        compiler_params=pltpu.CompilerParams(
            collective_id=0, has_side_effects=True, vmem_limit_bytes=60 * 1024 * 1024
        ),
        cost_estimate=pl.CostEstimate(flops=flops, bytes_accessed=6 << 20, transcendentals=0),
    )(activations, out_grads, moved_tiles, stale_roots)
    return tuple(pl.pallas_call(
        finish,
        out_shape=(
            jax.ShapeDtypeStruct((1,) + tile, BF16),
            jax.ShapeDtypeStruct((2, 2) + tile, BF16),
        ),
        in_specs=[
            pl.BlockSpec(memory_space=pl.ANY),
            pl.BlockSpec(memory_space=pl.ANY),
            pl.BlockSpec(memory_space=pltpu.VMEM),
        ],
        out_specs=(pl.BlockSpec(memory_space=pl.ANY), pl.BlockSpec(memory_space=pl.ANY)),
        scratch_shapes=[
            pltpu.VMEM(tile, F32),
            pltpu.VMEM((1,) + tile, BF16),
            pltpu.VMEM((2, 2) + tile, BF16),
            pltpu.SemaphoreType.DMA((12,)),
        ],
    )(precond, fresh, norm))


def solution(mesh):
    in_specs = (P("dp", "own"), P("dp", "own"), P("dp", "own"), P("dp", None, None, "own"))
    out_specs = (P("dp", None, "own"), P("dp", None, None, "own"))
    return jax.shard_map(body, mesh=mesh, in_specs=in_specs, out_specs=out_specs, check_vma=False)
```

```python
import functools

import jax
import jax.numpy as jnp
from jax import lax
from jax.experimental import pallas as pl
from jax.experimental.pallas import tpu as pltpu
from jax.sharding import PartitionSpec as P

N_DP = 32
N_OWN = 8
BS = 512
HALF = BS // 2
TOKENS = 16384
EPSILON = 1e-06
ENTRIES = N_DP * N_OWN * BS * BS

MESH = pl.DeviceIdType.MESH
F32 = jnp.float32
BF16 = jnp.bfloat16

X_ORDER = (0, 1, 3, 2)
SLICE = 128
SLICES = BS // SLICE
Y_PIECES = (
    (0, 1, 0, 128), (0, 1, 128, 128), (0, 1, 256, 128), (0, 1, 384, 128), (1, 3, 0, 128),
    (3, 4, 0, 128), (1, 4, 128, 64), (1, 4, 192, 64), (1, 4, 256, 64), (1, 4, 320, 64),
    (1, 4, 384, 64), (1, 4, 448, 64),
)
Z_PIECES = ((0, 64), (64, 64), (128, 64), (192, 64), (256, 64), (320, 64), (384, 64), (448, 64))

N_SEMS = 320


def dot(left, right, contract=(1, 0)):
    dims = (((contract[0],), (contract[1],)), ((), ()))
    return lax.dot_general(left, right, dims, preferred_element_type=F32)


def identity_rows(first_row, rows):
    row = lax.broadcasted_iota(jnp.int32, (rows, BS), 0) + first_row
    column = lax.broadcasted_iota(jnp.int32, (rows, BS), 1)
    return (row == column).astype(F32)


def kernel(
    act, grads, moved, stale,
    precond_out, fresh_out, norm_out,
    a_all, b_all, part,
    y_relay, y_sum, y_from_minus, y_from_plus,
    ysum,
    z_relay, z_sum, z_from_minus, z_from_plus,
    grad, grad_prev, flag, flag_prev, stale_v,
    left_applied, precond, stat, stat_b, mid_n, mid_e, mid_t, mid_tb,
    norm1, norm2, fresh,
    send_sems, recv_sems, local_sems,
):
    dp = lax.axis_index("dp")
    own = lax.axis_index("own")
    core = lax.rem(dp, 2)
    y = lax.rem(dp // 2, 4)
    z = dp // 8
    x = own // 2
    z_lo = lax.rem(own, 2)

    sibling = dp + 1 - 2 * core
    pair = own + 1 - 2 * z_lo
    x_plus, x_minus = lax.rem(own + 2, N_OWN), lax.rem(own + 6, N_OWN)

    def dp_y(by):
        return z * 8 + lax.rem(y + by, 4) * 2 + core

    def dp_at(by):
        return lax.rem(dp + by, N_DP)

    def dp_z(by):
        return dp_at(8 * by)

    def own_at(by):
        return lax.rem(own + by, N_OWN)

    sent = []
    counter = [0]
    my_tokens = pl.ds(pl.multiple_of(core * BS, BS), BS)
    sib_tokens = pl.ds(pl.multiple_of((1 - core) * BS, BS), BS)

    def new_sem():
        counter[0] += 1
        return counter[0] - 1

    def send(n, src, dst, to_dp, to_own, keep=True):
        copy = pltpu.make_async_remote_copy(
            src_ref=src, dst_ref=dst, send_sem=send_sems.at[n], recv_sem=recv_sems.at[n],
            device_id=(to_dp, to_own), device_id_type=MESH,
        )
        copy.start()
        if keep:
            sent.append((n, src.shape))

    def arrive(n, dst):
        pltpu.make_async_remote_copy(
            src_ref=dst, dst_ref=dst, send_sem=send_sems.at[n], recv_sem=recv_sems.at[n],
            device_id=(sibling, own), device_id_type=MESH,
        ).wait_recv()

    def features(part_of):
        return slice(part_of * SLICE, (part_of + 1) * SLICE)

    def block(r, part_of, tokens):
        return a_all.at[part_of, tokens, pl.ds(pl.multiple_of(r * SLICE, SLICE), SLICE)]

    def slab(at_x, part_of, tokens):
        return a_all.at[part_of, tokens, pl.ds(pl.multiple_of(at_x * 2 * SLICE, 2 * SLICE), 2 * SLICE)]

    def half_of(tokens, half):
        return pl.ds(pl.multiple_of(tokens.start + half * HALF, HALF), HALF)

    load_act = []
    for part_of in range(SLICES):
        load = pltpu.make_async_copy(act.at[:, features(part_of)], block(own, part_of, my_tokens), local_sems.at[4 + part_of])
        load.start()
        load_act.append(load)
    load_b = []
    for ch in range(2):
        load = pltpu.make_async_copy(
            grads.at[:, pl.ds(pl.multiple_of((2 * ch + core) * BS, BS), BS)],
            b_all.at[ch, pl.ds(pl.multiple_of(core * BS, BS), BS), :],
            local_sems.at[1 + ch],
        )
        load.start()
        load_b.append(load)
    load_stale = pltpu.make_async_copy(stale, stale_v, local_sems.at[3])
    load_stale.start()

    cross = lax.rem(dp + 2 * core - 1 + N_DP, N_DP)
    barrier = pltpu.get_barrier_semaphore()
    partners = [(dp, own_at(i)) for i in range(1, 8)]
    partners += [(sibling, own_at(i)) for i in range(N_OWN)]
    partners += [(dp_at(2 * i), own) for i in range(1, N_DP // 2)]
    partners += [(cross, own)]
    for partner in partners:
        pl.semaphore_signal(barrier, inc=1, device_id=partner, device_id_type=MESH)

    flag[...] = jnp.full((8, 128), moved[0, 0].astype(F32))

    pl.semaphore_wait(barrier, len(partners))

    n_flag = new_sem()
    n_b = [new_sem() for _ in range(2)]
    n_own = [new_sem() for _ in range(SLICES)]
    n_pair = [new_sem() for _ in range(SLICES)]
    next_dp = lax.rem(dp + 1, N_DP)
    for ch in range(2):
        send(
            n_b[ch],
            grads.at[:, pl.ds(pl.multiple_of((2 * ch + 1 - core) * BS, BS), BS)],
            b_all.at[ch, my_tokens, :],
            sibling, own,
        )
    n_first_up, n_first_down = new_sem(), new_sem()
    for part_of in range(SLICES):
        target = block(own, part_of, my_tokens)
        send(n_pair[part_of], act.at[:, features(part_of)], target, dp, pair)
        send(n_own[part_of], act.at[:, features(part_of)], target, sibling, own)
        if part_of == 0:
            send(n_first_up, act.at[:, features(0)], target, dp, x_plus)
            send(n_first_down, act.at[:, features(0)], target, dp, x_minus)
    send(n_flag, flag, flag_prev, next_dp, own)

    def products_here(r, part_of):
        for ch in range(2):
            target = lax.rem(lax.rem(r, 2) * 2 + ch - y + 4, 4)
            lanes = pl.ds(pl.multiple_of(r * SLICE, SLICE), SLICE)
            value = dot(a_all[part_of, :, lanes], b_all[ch], (0, 0)) * (1.0 / TOKENS)
            part[0, target, features(part_of), :] = value.astype(BF16)

    def products(part_of, first, last):
        rows = features(part_of)
        for ch in range(2):
            @pl.loop(first, last)
            def _(slot):
                at_x = lax.rem(x + slot + slot // 2 - 2 * (slot // 3), 4)
                lanes = pl.ds(pl.multiple_of(at_x * 2 * SLICE, 2 * SLICE), 2 * SLICE)
                value = dot(a_all[part_of, :, lanes], b_all[ch], (0, 0)) * (1.0 / TOKENS)
                value = value.astype(BF16)
                for parity in range(2):
                    target = lax.rem(2 * parity + ch - y + 4, 4)
                    part[slot, target, rows, :] = value[parity * SLICE:(parity + 1) * SLICE]

    for load in load_act + load_b:
        load.wait()
    for ch in range(2):
        arrive(n_b[ch], b_all.at[ch, sib_tokens, :])
    y_sems = [[new_sem() for _ in range(6)] for _ in Y_PIECES]
    z_sems = [[new_sem() for _ in range(6)] for _ in Z_PIECES]
    grad_sems = [new_sem() for _ in Z_PIECES]
    y_up, y_down = (dp_y(1), own), (dp_y(3), own)
    z_up, z_down = (dp_z(1), own), (dp_z(3), own)

    def cut(first, rows):
        middle = first + rows // 2
        return slice(first, middle), slice(middle, first + rows)

    in_first = [lax.rem(y + by, 4) // 2 == z_lo for by in range(4)]

    def y_far(piece, keep=True):
        start, stop, row, rows = Y_PIECES[piece]
        lo, hi = cut(row, rows)
        sems = y_sems[piece]
        send(sems[0], part.at[start:stop, 2, lo], y_relay.at[start:stop, lo], *y_up, keep=keep)
        send(sems[1], part.at[start:stop, 2, hi], y_relay.at[start:stop, hi], *y_down, keep=keep)

    def y_near(piece, by, keep=True):
        start, stop, row, rows = Y_PIECES[piece]
        lo, hi = cut(row, rows)
        sems = y_sems[piece]
        if by == 1:
            send(sems[2], part.at[start:stop, 1, hi], y_from_minus.at[start:stop, hi], *y_up, keep=keep)
        else:
            send(sems[3], part.at[start:stop, 3, lo], y_from_plus.at[start:stop, lo], *y_down, keep=keep)

    def y_dir(piece):
        y_near(piece, 1)
        y_near(piece, 3)

    def y_relayed(piece, by, keep=True):
        start, stop, row, rows = Y_PIECES[piece]
        lo, hi = cut(row, rows)
        slots = slice(start, stop)
        sems = y_sems[piece]
        rows, n, to, target = (lo, 0, y_up, y_from_minus) if by == 1 else (hi, 1, y_down, y_from_plus)
        arrive(sems[n], y_relay.at[slots, rows])
        y_sum[slots, rows] = part[slots, by, rows] + y_relay[slots, rows]
        send(sems[4 + n], y_sum.at[slots, rows], target.at[slots, rows], *to, keep=keep)

    def y_b(piece):
        y_relayed(piece, 1)
        y_relayed(piece, 3)

    def y_a_step(piece, first):
        pl.when(in_first[2] == first)(functools.partial(y_far, piece, first))
        for by in (1, 3):
            pl.when(in_first[by] == first)(functools.partial(y_near, piece, by, first))

    def y_b_step(piece, first):
        for by in (1, 3):
            pl.when(in_first[by] == first)(functools.partial(y_relayed, piece, by, first))

    def y_c(piece):
        start, stop, row, rows = Y_PIECES[piece]
        slots = slice(start, stop)
        lo, hi = cut(row, rows)
        sems = y_sems[piece]
        arrive(sems[2], y_from_minus.at[slots, hi])
        arrive(sems[3], y_from_plus.at[slots, lo])
        arrive(sems[4], y_from_minus.at[slots, lo])
        arrive(sems[5], y_from_plus.at[slots, hi])
        every = slice(row, row + rows)
        for slot in range(start, stop):
            total = part[slot, 0, every].astype(F32) + y_from_minus[slot, every].astype(F32)
            total = total + y_from_plus[slot, every].astype(F32)
            ysum[lax.rem(x + X_ORDER[slot] - z + 4, 4), every] = total.astype(BF16)

    def z_far(piece):
        lo, hi = cut(*Z_PIECES[piece])
        sems = z_sems[piece]
        send(sems[0], ysum.at[2, lo], z_relay.at[lo], *z_up)
        send(sems[1], ysum.at[2, hi], z_relay.at[hi], *z_down)

    def z_dir(piece):
        lo, hi = cut(*Z_PIECES[piece])
        sems = z_sems[piece]
        send(sems[2], ysum.at[1, hi], z_from_minus.at[hi], *z_up)
        send(sems[3], ysum.at[3, lo], z_from_plus.at[lo], *z_down)

    def z_b(piece):
        lo, hi = cut(*Z_PIECES[piece])
        sems = z_sems[piece]
        arrive(sems[0], z_relay.at[lo])
        z_sum[lo] = ysum[1, lo] + z_relay[lo]
        send(sems[4], z_sum.at[lo], z_from_minus.at[lo], *z_up)
        arrive(sems[1], z_relay.at[hi])
        z_sum[hi] = ysum[3, hi] + z_relay[hi]
        send(sems[5], z_sum.at[hi], z_from_plus.at[hi], *z_down)

    def z_c(piece):
        row, rows = Z_PIECES[piece]
        lo, hi = cut(row, rows)
        sems = z_sems[piece]
        arrive(sems[2], z_from_minus.at[hi])
        arrive(sems[3], z_from_plus.at[lo])
        arrive(sems[4], z_from_minus.at[lo])
        arrive(sems[5], z_from_plus.at[hi])
        every = slice(row, row + rows)
        total = ysum[0, every].astype(F32) + z_from_minus[every].astype(F32)
        total = total + z_from_plus[every].astype(F32)
        grad[every] = total.astype(BF16)

    def shift(piece):
        row, rows = Z_PIECES[piece]
        every = slice(row, row + rows)
        send(grad_sems[piece], grad.at[every], grad_prev.at[every], next_dp, own)

    x_next, x_prev, x_far = lax.rem(x + 1, 4), lax.rem(x + 3, 4), lax.rem(x + 2, 4)
    n_up = [new_sem() for _ in range(SLICES)]
    n_down = [new_sem() for _ in range(SLICES)]
    n_far = [[new_sem(), new_sem()] for _ in range(SLICES)]

    def give(src, to_dp, to_own):
        n = new_sem()
        send(n, src, src, to_dp, to_own)
        return n

    n_sib_pair, n_sib = {}, [[] for _ in range(SLICES)]

    def take_pair(part_of):
        arrive(n_pair[part_of], block(pair, part_of, my_tokens))
        n_sib_pair[part_of] = give(block(pair, part_of, my_tokens), sibling, own)

    def along_x(part_of):
        mine = block(pair, 0, my_tokens) if part_of == 0 else slab(x, part_of, my_tokens)
        send(n_up[part_of], mine, mine, dp, x_plus)
        send(n_down[part_of], mine, mine, dp, x_minus)

    def take_near(part_of):
        if part_of == 0:
            arrive(n_first_up, block(x_minus, 0, my_tokens))
            arrive(n_first_down, block(x_plus, 0, my_tokens))
        for n, at_x, half, to in ((n_up, x_prev, 0, x_plus), (n_down, x_next, 1, x_minus)):
            if part_of == 0:
                arrive(n[0], block(lax.rem(at_x * 2 + 1 - z_lo, N_OWN), 0, my_tokens))
            else:
                arrive(n[part_of], slab(at_x, part_of, my_tokens))
            onward = slab(at_x, part_of, half_of(my_tokens, half))
            send(n_far[part_of][half], onward, onward, dp, to)
            n_sib[part_of].append((give(slab(at_x, part_of, my_tokens), sibling, own), slab(at_x, part_of, sib_tokens)))

    def take_far(part_of):
        for half in range(2):
            arrive(n_far[part_of][half], slab(x_far, part_of, half_of(my_tokens, half)))
            n = give(slab(x_far, part_of, half_of(my_tokens, half)), sibling, own)
            n_sib[part_of].append((n, slab(x_far, part_of, half_of(sib_tokens, half))))

    def prod_own(part_of):
        arrive(n_own[part_of], block(own, part_of, sib_tokens))
        products_here(own, part_of)

    def prod_pair(part_of):
        arrive(n_sib_pair[part_of], block(pair, part_of, sib_tokens))
        products_here(pair, part_of)

    def prod_near(part_of):
        for n, ref in n_sib[part_of][:2]:
            arrive(n, ref)
        products(part_of, 1, 3)

    def prod_far(part_of):
        for n, ref in n_sib[part_of][2:]:
            arrive(n, ref)
        products(part_of, 3, 4)

    prod_own(0)
    y_a_step(0, True)
    prod_own(1)
    take_pair(0)
    y_a_step(1, True)
    along_x(0)
    prod_pair(0)
    y_a_step(0, False)
    prod_own(2)
    take_pair(1)
    along_x(1)
    y_a_step(2, True)
    prod_pair(1)
    y_a_step(1, False)
    take_pair(2)
    y_b_step(1, True)
    y_b_step(0, False)
    prod_own(3)
    take_near(0)
    prod_pair(2)
    y_b_step(0, True)
    y_a_step(2, False)
    y_a_step(3, True)
    prod_near(0)
    along_x(2)
    y_dir(4)
    take_near(1)
    y_b_step(1, False)
    y_far(4)
    y_c(0)
    take_far(0)
    y_b_step(2, True)
    prod_near(1)
    prod_far(0)
    take_pair(3)
    along_x(3)
    y_dir(5)
    y_far(5)
    take_near(2)
    y_b(4)
    prod_pair(3)
    take_far(1)
    prod_near(2)
    y_a_step(3, False)
    prod_far(1)
    y_b(5)
    y_far(7)
    y_dir(7)
    y_c(4)
    y_b_step(3, True)
    y_c(5)
    take_far(2)
    take_near(3)
    y_far(6)
    prod_far(2)
    y_b_step(2, False)
    y_far(9)
    prod_near(3)
    z_far(0)
    z_far(1)
    y_b(7)
    take_far(3)
    prod_far(3)
    y_dir(6)
    y_b(6)
    y_b_step(3, False)
    y_b(9)
    y_c(1)
    y_c(7)
    z_dir(0)
    y_dir(9)
    z_far(3)
    z_b(1)
    y_far(10)
    z_dir(1)
    y_far(8)
    z_b(0)
    y_c(2)
    z_dir(3)
    y_c(6)
    z_far(2)
    z_b(3)
    y_far(11)
    y_c(9)
    z_far(5)
    z_dir(5)
    y_c(3)
    y_dir(10)
    y_b(10)
    z_c(0)
    z_dir(2)
    y_b(11)
    y_dir(11)
    y_b(8)
    y_dir(8)
    z_b(5)
    z_b(2)
    y_c(10)
    z_far(6)
    z_dir(6)
    shift(0)
    y_c(11)
    z_dir(7)
    z_far(7)
    z_c(5)
    z_b(6)
    y_c(8)
    z_far(4)
    z_b(7)
    z_dir(4)
    z_c(3)
    z_c(1)
    z_b(4)
    z_c(6)
    shift(1)
    z_c(2)
    shift(3)
    shift(5)
    z_c(7)
    shift(7)
    shift(6)
    shift(2)
    z_c(4)
    shift(4)

    load_stale.wait()
    squares = jnp.zeros((1, 1), F32)
    for half in range(2):
        rows = slice(half * HALF, (half + 1) * HALF)
        left_applied[rows, :] = dot(stale_v[0, 0, rows, :], grad[...]).astype(BF16)
        value = dot(left_applied[rows, :], stale_v[0, 1])
        precond[rows, :] = value
        squares = squares + jnp.sum(value * value, keepdims=True)
    keep_precond = pltpu.make_async_copy(precond, precond_out, local_sems.at[0])
    keep_precond.start()

    def spread(store, value, targets):
        store[0] = jnp.broadcast_to(value, (8, 128))
        sems = [new_sem() for _ in targets]
        for i, target in enumerate(targets):
            send(sems[i], store.at[0], store.at[i + 1], *target)
        return sems

    def collect(store, sems):
        for i, n in enumerate(sems):
            arrive(n, store.at[i + 1])
        return jnp.sum(store[...], axis=0)[0:1, 0:1]

    def root(tile, side, slot, keep):
        total = jnp.zeros((1, 1), F32)
        for half in range(2):
            rows = slice(half * HALF, (half + 1) * HALF)
            if side == 0:
                value = dot(tile[rows, :], tile[...], (1, 1))
            else:
                value = dot(tile[:, rows], tile[...], (0, 0))
            value = value + EPSILON * identity_rows(half * HALF, HALF)
            stat[rows, :] = value
            total = total + jnp.sum(value * value, keepdims=True)
        scale = 2.5 / jnp.sqrt(total)
        stat_b[...] = (stat[...] * scale).astype(BF16)
        for half in range(2):
            rows = slice(half * HALF, (half + 1) * HALF)
            squared = dot(stat_b[rows, :], stat_b[...])
            matrix = stat[rows, :] * scale
            value = (5.0 * matrix - squared) * 0.25
            mid_n[rows, :] = value
            left_applied[rows, :] = value.astype(BF16)
            mid_e[rows, :] = ((squared - 10.0 * matrix) * 0.0625).astype(BF16)
        for half in range(2):
            rows = slice(half * HALF, (half + 1) * HALF)
            value = 1.5625 * mid_n[rows, :] + dot(mid_e[rows, :], left_applied[...])
            mid_t[rows, :] = value
            mid_tb[rows, :] = value.astype(BF16)
        factor = jnp.sqrt(jnp.sqrt(scale)) * 0.25
        for half in range(2):
            rows = slice(half * HALF, (half + 1) * HALF)
            value = 1.5625 * mid_t[rows, :] + dot(mid_e[rows, :], mid_tb[...])
            first = (25.0 * identity_rows(half * HALF, HALF) - 5.0 * (stat[rows, :] * scale)) * 0.25
            result = ((first - value) * factor).astype(BF16)
            fresh[slot, side, rows, :] = (result.astype(F32) * keep).astype(BF16)

    keep_fresh = []

    def keep_root(slot, side):
        copy = pltpu.make_async_copy(fresh.at[slot, side], fresh_out.at[slot, side], local_sems.at[4 + 2 * slot + side])
        copy.start()
        keep_fresh.append(copy)

    near = [(dp, own_at(i)) for i in range(1, N_OWN)] + [(sibling, own_at(i)) for i in range(N_OWN)]
    sems1 = spread(norm1, squares, near)
    keep = 1.0 - flag[0:1, 0:1]
    root(grad, 0, 0, keep)
    keep_root(0, 0)
    sems2 = spread(norm2, collect(norm1, sems1), [(dp_at(2 * i), own) for i in range(1, N_DP // 2)])
    root(grad, 1, 0, keep)
    keep_root(0, 1)
    arrive(n_flag, flag_prev)
    for n, (row, rows) in zip(grad_sems, Z_PIECES):
        arrive(n, grad_prev.at[row:row + rows])
    keep = flag_prev[0:1, 0:1]
    for side in range(2):
        root(grad_prev, side, 1, keep)
        keep_root(1, side)
    norm_out[...] = jnp.broadcast_to(collect(norm2, sems2), (8, 128))

    for copy in keep_fresh:
        copy.wait()
    keep_precond.wait()
    for n, shape in sent:
        if shape[0] == 8:
            ref = norm1.at[0]
        elif len(shape) == 2:
            ref = part.at[0, 0, 0:shape[0], 0:shape[1]]
        else:
            ref = part.at[0:shape[0], 0, 0:shape[1]]
        pltpu.make_async_remote_copy(
            src_ref=ref, dst_ref=ref, send_sem=send_sems.at[n], recv_sem=recv_sems.at[n],
            device_id=(sibling, own), device_id_type=MESH,
        ).wait_send()
    assert counter[0] <= N_SEMS, counter[0]


def finish(precond, fresh, norm, update, fresh_out, value, result, roots, sems):
    tiles = [(slot, side) for slot in range(2) for side in range(2)]
    halves = [slice(half * HALF, (half + 1) * HALF) for half in range(2)]
    loads = [pltpu.make_async_copy(fresh.at[t], roots.at[t], sems.at[i]) for i, t in enumerate(tiles)]
    stores = [pltpu.make_async_copy(roots.at[t], fresh_out.at[t], sems.at[4 + i]) for i, t in enumerate(tiles)]
    values = [pltpu.make_async_copy(precond.at[h], value.at[h], sems.at[8 + i]) for i, h in enumerate(halves)]
    results = [pltpu.make_async_copy(result.at[0, h], update.at[0, h], sems.at[10 + i]) for i, h in enumerate(halves)]
    for copy in loads + values:
        copy.start()
    scale = lax.rsqrt(norm[0:1, 0:1] / ENTRIES + 1e-06)
    for arrived, leave in zip(loads, stores):
        arrived.wait()
        leave.start()
    for rows, arrived, leave in zip(halves, values, results):
        arrived.wait()
        result[0, rows] = (value[rows] * scale).astype(BF16)
        leave.start()
    for copy in stores + results:
        copy.wait()


def body(activations, out_grads, moved_tiles, stale_roots):
    tile = (BS, BS)
    scratch = [
        ((SLICES, 2 * BS, N_OWN * SLICE), BF16),
        ((2, 2 * BS, BS), BF16),
        ((4, 4) + tile, BF16),
        ((4,) + tile, BF16), ((4,) + tile, BF16), ((4,) + tile, BF16), ((4,) + tile, BF16),
        ((4,) + tile, BF16),
        (tile, BF16), (tile, BF16), (tile, BF16), (tile, BF16),
        (tile, BF16), (tile, BF16), ((8, 128), F32), ((8, 128), F32), ((1, 2) + tile, BF16),
        (tile, BF16), (tile, F32), (tile, F32), (tile, BF16), (tile, F32), (tile, BF16),
        (tile, F32), (tile, BF16),
        ((2 * N_OWN, 8, 128), F32), ((N_DP // 2, 8, 128), F32), ((2, 2) + tile, BF16),
    ]
    flops = 2 * 2 * 512 * 4096 * 2048
    precond, fresh, norm = pl.pallas_call(
        kernel,
        out_shape=(
            jax.ShapeDtypeStruct(tile, F32),
            jax.ShapeDtypeStruct((2, 2) + tile, BF16),
            jax.ShapeDtypeStruct((8, 128), F32),
        ),
        in_specs=[
            pl.BlockSpec(memory_space=pl.ANY),
            pl.BlockSpec(memory_space=pl.ANY),
            pl.BlockSpec(memory_space=pltpu.SMEM),
            pl.BlockSpec(memory_space=pl.ANY),
        ],
        out_specs=(
            pl.BlockSpec(memory_space=pl.ANY),
            pl.BlockSpec(memory_space=pl.ANY),
            pl.BlockSpec(memory_space=pltpu.VMEM),
        ),
        scratch_shapes=[pltpu.VMEM(shape, dtype) for shape, dtype in scratch] + [
            pltpu.SemaphoreType.DMA((N_SEMS,)),
            pltpu.SemaphoreType.DMA((N_SEMS,)),
            pltpu.SemaphoreType.DMA((4 + SLICES,)),
        ],
        compiler_params=pltpu.CompilerParams(
            collective_id=0, has_side_effects=True, vmem_limit_bytes=60 * 1024 * 1024
        ),
        cost_estimate=pl.CostEstimate(flops=flops, bytes_accessed=6 << 20, transcendentals=0),
    )(activations, out_grads, moved_tiles, stale_roots)
    return tuple(pl.pallas_call(
        finish,
        out_shape=(
            jax.ShapeDtypeStruct((1,) + tile, BF16),
            jax.ShapeDtypeStruct((2, 2) + tile, BF16),
        ),
        in_specs=[
            pl.BlockSpec(memory_space=pl.ANY),
            pl.BlockSpec(memory_space=pl.ANY),
            pl.BlockSpec(memory_space=pltpu.VMEM),
        ],
        out_specs=(pl.BlockSpec(memory_space=pl.ANY), pl.BlockSpec(memory_space=pl.ANY)),
        scratch_shapes=[
            pltpu.VMEM(tile, F32),
            pltpu.VMEM((1,) + tile, BF16),
            pltpu.VMEM((2, 2) + tile, BF16),
            pltpu.SemaphoreType.DMA((12,)),
        ],
    )(precond, fresh, norm))


def solution(mesh):
    in_specs = (P("dp", "own"), P("dp", "own"), P("dp", "own"), P("dp", None, None, "own"))
    out_specs = (P("dp", None, "own"), P("dp", None, None, "own"))
    return jax.shard_map(body, mesh=mesh, in_specs=in_specs, out_specs=out_specs, check_vma=False)
```
